128 devices in a mesh: lat: 16 (over z, x_hi, core), lon: 8 (over x_lo, y).
Axes of the slice: x: 4 (x_hi: 2, x_lo: 2; x = x_hi * 2 + x_lo), y: 4, z: 4, core: 2. Of those that a mesh axis runs over, the one named last changes fastest.
Arguments:
- grid_feat: bfloat16 [32, 16, 128, 474], P('lat', 'lon'), may hold values from -40 to 40
- mesh_feat: bfloat16 [16, 8, 3, 384], P('lat', 'lon'), may hold values from -1 to 1
- g2m_feat: bfloat16 [16, 8, 6, 4, 128], P('lat', 'lon'), may hold values from -4 to 4
- g2m_src: int32 [16, 8, 6], P('lat', 'lon'), may hold values from 0 to 15
- g2m_dst: int32 [16, 8, 6], P('lat', 'lon'), may hold values from 0 to 2
- g2m_rows: int32 [16, 8, 6, 2, 128], P('lat', 'lon'), may hold values from 0 to 127
- g2m_mask: int32 [16, 8, 6, 128], P('lat', 'lon'), may hold values 0 or 1
- g2m_live: int32 [16, 8], P('lat', 'lon'), may hold values from 1 to 6, as said below
- mesh_efeat: bfloat16 [16, 8, 24, 4, 128], P('lat', 'lon'), may hold values from -4 to 4
- mesh_src: int32 [16, 8, 24], P('lat', 'lon'), may hold values from 0 to 34
- mesh_dst: int32 [16, 8, 24], P('lat', 'lon'), may hold values from 0 to 2
- mesh_rows: int32 [16, 8, 24, 2, 128], P('lat', 'lon'), may hold values from 0 to 127
- mesh_mask: int32 [16, 8, 24, 128], P('lat', 'lon'), may hold values 0 or 1
- grid_in: bfloat16 [474, 512], replicated, may hold values from -0.25 to 0.25
- mesh_in: bfloat16 [3, 512], replicated, may hold values from -3.5 to 3.5
- edge_in: bfloat16 [2, 4, 512], replicated, may hold values from -3 to 3
- edge_first: bfloat16 [2, 1536, 512], replicated, may hold values from -0.15625 to 0.15625
- node_first: bfloat16 [2, 1024, 512], replicated, may hold values from -0.1875 to 0.1875
- second: bfloat16 [8, 512, 512], replicated, may hold values from -0.25 to 0.25
- norm_gains: bfloat16 [8, 512], replicated, may hold values from 0.099609375 to 1.8984375
Outputs:
- mesh_out: bfloat16 [16, 8, 384, 512], P('lat', 'lon')
The draws below stay inside these ranges and needn't reach their ends.
Inputs may be any that keep to these rules, and one draw needn't show every extreme that they name: `g2m_live`: the bands at both poles have all 6 block pairs live.
All inputs are finite; a program needn't handle non-finite values. No bound on the sum of `g2m_mask` or of `mesh_mask` on one device may be relied on, other than what follows from the above.
Results may differ from the reference program's by a relative error of at most 0.015.
Values may be sent and summed in bfloat16 or wider, within the bound.
A program may use at most 64 MiB of HBM per device.

```python
import jax
import jax.numpy as jnp
from jax import lax

LATENT = 512
GRID_IN = 474
MESH_IN = 3
EDGE_IN = 4
BLK = 128
E_BLK = 128
BLAT = 2
BLON = 2
MB_DEV = 3
COARSE_DEV = 8
G2M_CAP = 6
M_CAP = 24
BANDS = 16
SECTORS = 8
GLAT = 32
GLON = 16
MROWS = 384
GRID_SRC = 16
MESH_SRC = 35
N_LAT = 16
N_LON = 8


def draw_grid_feat(key, part):
    key = jax.random.fold_in(key, 5)
    key_base, key_node, key_column = jax.random.split(key, 3)
    shape = (GLAT, GLON, BLK, GRID_IN)
    node_scale = jnp.exp(jax.random.uniform(key_node, (GLAT, GLON, BLK, 1), jnp.float32, 0.0, 1.1513))
    column_scale = jnp.exp(jax.random.uniform(key_column, (GRID_IN,), jnp.float32, 0.0, 1.1513))
    base_values = jnp.clip(jax.random.normal(key_base, shape, jnp.float32), -4.0, 4.0)
    return (base_values * node_scale * column_scale).astype(jnp.bfloat16)


def draw_g2m_live(key, part):
    key = jax.random.fold_in(key, 11)
    band_number = jnp.arange(BANDS, dtype=jnp.int32)
    distance = jnp.abs(2 * band_number - (BANDS - 1))
    lowest = G2M_CAP // 6
    base_count = lowest + (G2M_CAP - lowest) * distance * distance // ((BANDS - 1) * (BANDS - 1))
    jitter = jax.random.randint(key, (BANDS, SECTORS), 0, 2, dtype=jnp.int32)
    return jnp.minimum(base_count[:, None] + jitter, G2M_CAP).astype(jnp.int32)


def plant(values, own_key, least, high):
    longest = values.shape.index(max(values.shape))
    spots = []
    for shift in (0, 1):
        where = [jax.random.randint(jax.random.fold_in(own_key, axis), (), 0, length) for axis, length in enumerate(values.shape)]
        where[longest] = (where[longest] + shift) % values.shape[longest]
        spots.append(tuple(where))
    return values.at[spots[0]].set(least).at[spots[1]].set(high)


def block_scale(rng, extent, pieces, least, largest):
    def one(position, blocks):
        draws = jax.random.uniform(jax.random.fold_in(jax.random.fold_in(rng, 6), position), (blocks,), jnp.float32, least / len(pieces), largest / len(pieces))
        return jnp.repeat(jnp.exp(draws), extent[position] // blocks).reshape((-1,) + (1,) * (len(extent) - position - 1))

    gain = one(*pieces[0])
    for cut in pieces[1:]:
        gain = gain * one(*cut)
    return gain


def scatter_about(own_key, shape, width, bound, cuts=(), kind=jnp.bfloat16):
    factor_of = block_scale(own_key, shape, cuts, -0.22, 0.18) if cuts else 1.0
    drawn = jax.random.normal(own_key, shape, jnp.float32) * width * factor_of
    return jnp.minimum(jnp.maximum(drawn, -bound), bound).astype(kind)


def setup_inputs(seed: int = 0) -> dict:
    keys = jax.random.split(jax.random.key(seed), 21)
    grid_feat = draw_grid_feat(jax.random.fold_in(keys[20], 71), 0)
    mesh_feat = jnp.clip(jax.random.uniform(keys[1], (BANDS, SECTORS, MESH_IN, MROWS), jnp.float32, -1.0, 1.0) * block_scale(keys[1], (BANDS, SECTORS, MESH_IN, MROWS), ((0, 16), (1, 8)), -0.4, 0.0), -1.0, 1.0).astype(jnp.bfloat16)
    g2m_feat = scatter_about(keys[2], (BANDS, SECTORS, G2M_CAP, EDGE_IN, E_BLK), 1.0, 4.0, ((0, 16), (1, 8)))
    g2m_src = plant(jax.random.randint(keys[3], (BANDS, SECTORS, G2M_CAP), 0, GRID_SRC), jax.random.fold_in(keys[3], 1), 0, GRID_SRC - 1).astype(jnp.int32)
    g2m_dst = plant(jax.random.randint(keys[4], (BANDS, SECTORS, G2M_CAP), 0, MB_DEV), jax.random.fold_in(keys[4], 1), 0, MB_DEV - 1).astype(jnp.int32)
    g2m_rows = plant(jax.random.randint(keys[5], (BANDS, SECTORS, G2M_CAP, 2, E_BLK), 0, BLK), jax.random.fold_in(keys[5], 1), 0, BLK - 1).astype(jnp.int32)
    g2m_mask = plant((jax.random.randint(keys[6], (BANDS, SECTORS, G2M_CAP, E_BLK), 0, 5) < 4).astype(jnp.int32), jax.random.fold_in(keys[6], 1), 0, 1)
    g2m_live = draw_g2m_live(jax.random.fold_in(keys[20], 71), 0)
    mesh_efeat = scatter_about(keys[8], (BANDS, SECTORS, M_CAP, EDGE_IN, E_BLK), 1.0, 4.0, ((0, 16), (1, 8)))
    mesh_src = plant(jax.random.randint(keys[9], (BANDS, SECTORS, M_CAP), 0, MESH_SRC), jax.random.fold_in(keys[9], 1), 0, MESH_SRC - 1).astype(jnp.int32)
    mesh_dst = plant(jax.random.randint(keys[10], (BANDS, SECTORS, M_CAP), 0, MB_DEV), jax.random.fold_in(keys[10], 1), 0, MB_DEV - 1).astype(jnp.int32)
    mesh_rows = plant(jax.random.randint(keys[11], (BANDS, SECTORS, M_CAP, 2, E_BLK), 0, BLK), jax.random.fold_in(keys[11], 1), 0, BLK - 1).astype(jnp.int32)
    mesh_mask = plant((jax.random.randint(keys[12], (BANDS, SECTORS, M_CAP, E_BLK), 0, 10) < 9).astype(jnp.int32), jax.random.fold_in(keys[12], 1), 0, 1)
    grid_in = scatter_about(keys[13], (GRID_IN, LATENT), GRID_IN ** -0.5, 0.25)
    mesh_in = scatter_about(keys[14], (MESH_IN, LATENT), MESH_IN ** -0.5, 3.5)
    edge_in = scatter_about(keys[15], (2, EDGE_IN, LATENT), EDGE_IN ** -0.5, 3.0)
    edge_first = scatter_about(keys[16], (2, 3 * LATENT, LATENT), (3 * LATENT) ** -0.5, 0.15625)
    node_first = scatter_about(keys[17], (2, 2 * LATENT, LATENT), (2 * LATENT) ** -0.5, 0.1875)
    second = scatter_about(keys[18], (8, LATENT, LATENT), LATENT ** -0.5, 0.25)
    norm_gains = jnp.clip(1.0 + 0.18 * jax.random.normal(keys[19], (8, LATENT), jnp.float32), 0.099609375, 1.8984375).astype(jnp.bfloat16)
    return {"grid_feat": grid_feat, "mesh_feat": mesh_feat, "g2m_feat": g2m_feat, "g2m_src": g2m_src, "g2m_dst": g2m_dst, "g2m_rows": g2m_rows, "g2m_mask": g2m_mask, "g2m_live": g2m_live, "mesh_efeat": mesh_efeat, "mesh_src": mesh_src, "mesh_dst": mesh_dst, "mesh_rows": mesh_rows, "mesh_mask": mesh_mask, "grid_in": grid_in, "mesh_in": mesh_in, "edge_in": edge_in, "edge_first": edge_first, "node_first": node_first, "second": second, "norm_gains": norm_gains}


def perceptron(inputs, first_weight, second_weight, gain_row):
    hidden = jax.nn.silu(jnp.dot(inputs, first_weight, preferred_element_type=jnp.float32)).astype(jnp.bfloat16)
    outputs = jnp.dot(hidden, second_weight, preferred_element_type=jnp.float32)
    centred = outputs - lax.optimization_barrier(jnp.mean(outputs, axis=-1, keepdims=True))
    spread = lax.optimization_barrier(jnp.mean(centred * centred, axis=-1, keepdims=True))
    return centred * lax.rsqrt(spread + 1e-05) * gain_row.astype(jnp.float32)

def block_messages(source_block, target_block, features, row_pair, weighting, edge_weight, update_weight, embed_second, embed_gain, update_second, update_gain):
    positions = jnp.arange(source_block.shape[0], dtype=jnp.int32)
    pick_source = (row_pair[0][:, None] == positions[None, :]).astype(jnp.bfloat16)
    pick_target = (row_pair[1][:, None] == positions[None, :]).astype(jnp.bfloat16)
    edge_start = perceptron(features.T, edge_weight, embed_second, embed_gain).astype(jnp.bfloat16)
    source_rows = jnp.dot(pick_source, source_block, preferred_element_type=jnp.float32).astype(jnp.bfloat16)
    target_rows = jnp.dot(pick_target, target_block, preferred_element_type=jnp.float32).astype(jnp.bfloat16)
    joined = jnp.concatenate([edge_start, source_rows, target_rows], axis=1)
    updated = edge_start.astype(jnp.float32) + perceptron(joined, update_weight, update_second, update_gain)
    message = (updated * weighting[:, None]).astype(jnp.bfloat16)
    return jnp.dot(pick_target.T, message, preferred_element_type=jnp.float32)

def surround(field):
    padded = jnp.pad(field, ((1, 1), (0, 0), (0, 0), (0, 0)))
    return jnp.concatenate([padded[:, -1:], padded, padded[:, :1]], axis=1)

def reference(grid_feat, mesh_feat, g2m_feat, g2m_src, g2m_dst, g2m_rows, g2m_mask, g2m_live, mesh_efeat, mesh_src, mesh_dst, mesh_rows, mesh_mask, grid_in, mesh_in, edge_in, edge_first, node_first, second, norm_gains):
    grid_latent = perceptron(grid_feat, grid_in, second[0], norm_gains[0]).astype(jnp.bfloat16)
    grid_around = surround(grid_latent)
    mesh_start = perceptron(jnp.swapaxes(mesh_feat, 2, 3), mesh_in, second[1], norm_gains[1]).astype(jnp.bfloat16)
    anchor = jnp.int32(0)

    def encode(device):
        band_index = (device // N_LON).astype(jnp.int32)
        sector = (device % N_LON).astype(jnp.int32)
        starts = ((band_index * BLAT).astype(jnp.int32), (sector * BLON).astype(jnp.int32), anchor, anchor)
        source_table = lax.dynamic_slice(grid_around, starts, (BLAT + 2, BLON + 2, BLK, LATENT)).reshape(-1, BLK, LATENT)
        targets = mesh_start[band_index, sector].reshape(MB_DEV, BLK, LATENT)

        def add_slot(slot_index, running):
            target_index = g2m_dst[band_index, sector, slot_index]
            block_sum = block_messages(source_table[g2m_src[band_index, sector, slot_index]], targets[target_index], g2m_feat[band_index, sector, slot_index], g2m_rows[band_index, sector, slot_index], g2m_mask[band_index, sector, slot_index].astype(jnp.float32), edge_in[0], edge_first[0], second[2], norm_gains[2], second[4], norm_gains[4])
            return running.at[target_index].add(block_sum)
        return lax.fori_loop(jnp.int32(0), g2m_live[band_index, sector].astype(jnp.int32), add_slot, jnp.zeros((MB_DEV, BLK, LATENT), jnp.float32))
    g2m_sum = lax.map(encode, jnp.arange(N_LAT * N_LON, dtype=jnp.int32)).reshape(N_LAT, N_LON, MROWS, LATENT)
    g2m_round = g2m_sum.astype(jnp.bfloat16)
    mesh_one = (mesh_start.astype(jnp.float32) + perceptron(jnp.concatenate([mesh_start, g2m_round], axis=-1), node_first[0], second[6], norm_gains[6])).astype(jnp.bfloat16)
    mesh_around = surround(mesh_one)
    coarse_table = mesh_one[:, :, :COARSE_DEV, :].reshape(-1, BLK, LATENT)

    def process(device):
        band_index = (device // N_LON).astype(jnp.int32)
        sector = (device % N_LON).astype(jnp.int32)
        starts = (band_index, sector, anchor, anchor)
        near_blocks = lax.dynamic_slice(mesh_around, starts, (3, 3, MROWS, LATENT)).reshape(-1, BLK, LATENT)
        source_table = jnp.concatenate([near_blocks, coarse_table], axis=0)
        targets = mesh_one[band_index, sector].reshape(MB_DEV, BLK, LATENT)

        def add_slot(slot_index, running):
            target_index = mesh_dst[band_index, sector, slot_index]
            block_sum = block_messages(source_table[mesh_src[band_index, sector, slot_index]], targets[target_index], mesh_efeat[band_index, sector, slot_index], mesh_rows[band_index, sector, slot_index], mesh_mask[band_index, sector, slot_index].astype(jnp.float32), edge_in[1], edge_first[1], second[3], norm_gains[3], second[5], norm_gains[5])
            return running.at[target_index].add(block_sum)
        return lax.fori_loop(jnp.int32(0), jnp.int32(M_CAP), add_slot, jnp.zeros((MB_DEV, BLK, LATENT), jnp.float32))
    mesh_sum = lax.map(process, jnp.arange(N_LAT * N_LON, dtype=jnp.int32)).reshape(N_LAT, N_LON, MROWS, LATENT)
    mesh_round = mesh_sum.astype(jnp.bfloat16)
    return (mesh_one.astype(jnp.float32) + perceptron(jnp.concatenate([mesh_one, mesh_round], axis=-1), node_first[1], second[7], norm_gains[7])).astype(jnp.bfloat16)
```

```python
import functools

import jax
import jax.numpy as jnp
from jax import lax
from jax.experimental import pallas as pl
from jax.experimental.pallas import tpu as pltpu
from jax.sharding import PartitionSpec as P

BF = jnp.bfloat16
F32 = jnp.float32
MESH = pl.DeviceIdType.MESH
BLK = 128
GROUP = 4
GGROUP = 3
EARLY = 2
NEAR = 27
COARSE = 8


def mm(a, b):
    return jnp.dot(a, b, preferred_element_type=F32)


def silu(x):
    half = 0.5 * x
    return (half * jnp.tanh(half) + half).astype(BF)


def unit_rows(v):
    return v * lax.rsqrt(jnp.mean(v * v, axis=-1, keepdims=True) + 1e-05)


def kernel(
    grid_feat,
    grid_in,
    second,
    edge_first,
    node_first,
    mesh_feat,
    g2m_feat,
    g2m_rows,
    g2m_mask,
    mesh_efeat,
    mesh_rows,
    mesh_mask,
    mesh_in,
    edge_in,
    norm_gains,
    g2m_src,
    g2m_dst,
    g2m_live,
    mesh_src,
    mesh_dst,
    out,
    feat_v,
    gin_v,
    sec_v,
    ef_v,
    nf_v,
    gt,
    mt,
    start_v,
    one_v,
    dproj,
    npre,
    g_pre,
    g_pick,
    g_scat,
    m_pre,
    m_pick,
    m_scat,
    acc_e,
    acc_m,
    acc_g,
    acc_h,
    load_sem,
    send_sem,
    recv_sem,
):
    lat, lon = lax.axis_index("lat"), lax.axis_index("lon")
    n_lat, n_lon = lax.axis_size("lat"), lax.axis_size("lon")
    par = lax.rem(lat, 2)
    chip = lat // 2
    east = (lat, lax.rem(lon + 1, n_lon))
    west = (lat, lax.rem(lon + n_lon - 1, n_lon))
    twin = (lat + 1 - 2 * par, lon)
    far_lat = lat + 2 * par - 1
    has_far = jnp.logical_and(far_lat >= 0, far_lat < n_lat)
    far = (far_lat, lon)
    lon_mates = [(lat, lax.rem(lon + t, n_lon)) for t in range(1, n_lon)]
    x_mate = (lat + 2 - 4 * lax.rem(chip, 2), lon)
    z_mates = [(lax.rem(lat + 4 * t, n_lat), lon) for t in range(1, n_lat // 4)]

    loads = {}

    def load(name, src, dst):
        copy = pltpu.make_async_copy(src, dst, load_sem.at[len(loads)])
        copy.start()
        loads[name] = copy

    def loaded(*names):
        for name in names:
            loads[name].wait()

    load("feat", grid_feat, feat_v)
    load("gin", grid_in, gin_v)
    load("s0", second.at[0], sec_v.at[0])
    load("e0", edge_first.at[0], ef_v.at[0])
    load("s1", second.at[1], sec_v.at[1])
    load("s2", second.at[2], sec_v.at[2])
    load("n0", node_first.at[0], nf_v.at[0])
    load("s3", second.at[3], sec_v.at[3])
    load("e1", edge_first.at[1], ef_v.at[1])
    load("s4", second.at[4], sec_v.at[4])
    load("s6", second.at[6], sec_v.at[6])
    load("s5", second.at[5], sec_v.at[5])
    load("n1", node_first.at[1], nf_v.at[1])
    load("s7", second.at[7], sec_v.at[7])

    barrier = pltpu.get_barrier_semaphore()
    mates = lon_mates + [twin, x_mate] + z_mates
    for mate in mates:
        pl.semaphore_signal(barrier, inc=1, device_id=mate, device_id_type=MESH)

    @pl.when(has_far)
    def _():
        pl.semaphore_signal(barrier, inc=1, device_id=far, device_id_type=MESH)

    gains = norm_gains[...].astype(F32)

    def gain(k):
        return gains[k : k + 1]

    def centre(k):
        w = sec_v[k].astype(F32)
        sec_v[k] = (w - jnp.mean(w, axis=-1, keepdims=True)).astype(BF)

    numbers = {}

    def remote(name, src, dst, device):
        index = numbers.setdefault(name, len(numbers))
        return pltpu.make_async_remote_copy(
            src_ref=src,
            dst_ref=dst,
            send_sem=send_sem.at[index],
            recv_sem=recv_sem.at[index],
            device_id=device,
            device_id_type=MESH,
        )

    def g_at(r, c, n=1):
        return gt.at[pl.ds(r * 4 + c, n)]

    on_row, off_row = 3 * (1 - par), 3 * par
    g_rows = (1 + par, 2 - par)
    g_copies = {}
    for t in range(2):
        g_copies["e", t] = remote(("ge", t), g_at(g_rows[t], 2), g_at(g_rows[t], 0), east)
        g_copies["w", t] = remote(("gw", t), g_at(g_rows[t], 1), g_at(g_rows[t], 3), west)
    g_copies["far"] = remote("gfar", g_at(g_rows[0], 1, 2), g_at(on_row, 1, 2), far)
    g_copies["twin"] = remote("gtwin", g_at(g_rows[1], 1, 2), g_at(off_row, 1, 2), twin)
    g_copies["far_e"] = remote("gfe", g_at(off_row, 2), g_at(off_row, 0), east)
    g_copies["far_w"] = remote("gfw", g_at(off_row, 1), g_at(off_row, 3), west)
    g_copies["twin_e"] = remote("gte", g_at(g_rows[1], 0), g_at(off_row, 0), twin)
    g_copies["twin_w"] = remote("gtw", g_at(g_rows[1], 3), g_at(off_row, 3), twin)

    @pl.when(jnp.logical_not(has_far))
    def _():
        gt[pl.ds(off_row * 4, 4)] = jnp.zeros((4, BLK, 512), BF)
        mt[pl.ds(2 * par * 9, 9)] = jnp.zeros((9, BLK, 512), BF)

    loaded("feat", "gin", "s0")
    centre(0)
    w_in = gin_v[...]
    for t in range(2):
        x = feat_v[g_rows[t] - 1].reshape(2 * BLK, -1)
        v = mm(silu(mm(x, w_in)), sec_v[0])
        latent = (unit_rows(v) * gain(0)).astype(BF)
        if t == 0:
            loaded("e0")
        proj = mm(latent, ef_v[0, 512:1024]).astype(BF)
        gt[pl.ds(g_rows[t] * 4 + 1, 2)] = proj.reshape(2, BLK, 512)
        if t == 0:
            pl.semaphore_wait(barrier, len(mates) + jnp.where(has_far, 1, 0))

            @pl.when(has_far)
            def _():
                g_copies["far"].start()

        else:
            g_copies["twin"].start()
        g_copies["e", t].start()
        g_copies["w", t].start()

    loaded("s1")
    centre(1)
    u = lax.dot_general(
        mesh_feat[0, 0], mesh_in[...], (((0,), (0,)), ((), ())), preferred_element_type=F32
    )
    start = (unit_rows(mm(silu(u), sec_v[1])) * gain(1)).astype(BF)
    start_v[...] = start
    dproj[...] = mm(start, ef_v[0, 1024:1536]).astype(BF).reshape(3, BLK, 512)
    loaded("n0")
    npre[...] = mm(start, nf_v[0, 0:512])

    def embed(base, count, feat, rows, mask, src, dst, live, layer, k, pre, pick, scat, acc, far_blocks):
        w_edge = edge_in[layer]
        hidden = []
        scatters = []
        spot = lax.broadcasted_iota(jnp.int32, (BLK, BLK), 0)
        place = lax.broadcasted_iota(jnp.int32, (3 * BLK, BLK), 0)
        for q in range(count):
            s = base + q
            u = lax.dot_general(
                feat[0, 0, s], w_edge, (((0,), (0,)), ((), ())), preferred_element_type=F32
            )
            hidden.append(silu(u))
            pair = rows[0, 0, s]
            hs, hd = pair[0:1], pair[1:2]
            if far_blocks:
                moved = ((hs >> 3) & 7) * 16 + (hs >> 6) * 8 + (hs & 7)
                is_coarse = jnp.where(src[0, 0, s] >= NEAR, 1, 0)
                hs = hs + is_coarse * (moved - hs)
            pick_s = jnp.where(spot == hs, 1.0, 0.0).T.astype(BF)
            pick_d = jnp.where(spot == hd, 1.0, 0.0).T.astype(BF)
            pick[s] = jnp.concatenate([pick_s, pick_d], axis=1)
            keep = mask[0, 0, pl.ds(s, 1), :]
            if live is not None:
                keep = keep * jnp.where(s < live, 1, 0)
            target = jnp.where(keep != 0, hd + BLK * dst[0, 0, s], -1)
            one = jnp.where(place == target, 1.0, 0.0).astype(BF)
            scat[s] = one
            scatters.append(one)
        e = (unit_rows(mm(jnp.concatenate(hidden, axis=0), sec_v[k])) * gain(k)).astype(BF)
        pre[pl.ds(base, count)] = mm(e, ef_v[layer, 0:512]).reshape(count, BLK, 512)
        acc[...] += mm(jnp.concatenate(scatters, axis=1), e)

    def update(base, count, src, dst, k, pre, pick, scat, table, acc):
        hidden = []
        for q in range(count):
            s = base + q
            blocks = jnp.concatenate([table[src[0, 0, s]], dproj[dst[0, 0, s]]], axis=0)
            hidden.append(silu(pre[s] + mm(pick[s], blocks)))
        message = unit_rows(mm(jnp.concatenate(hidden, axis=0), sec_v[k])).astype(BF)
        scatters = jnp.concatenate([scat[base + q] for q in range(count)], axis=1)
        acc[...] += mm(scatters, message)

    zeros = jnp.zeros(acc_e.shape, F32)
    acc_e[...] = zeros
    acc_m[...] = zeros
    acc_g[...] = zeros
    acc_h[...] = zeros
    live = g2m_live[0, 0]
    loaded("s2")
    centre(2)

    @pl.loop(0, 6 // GGROUP)
    def _(n):
        embed(
            n * GGROUP, GGROUP, g2m_feat, g2m_rows, g2m_mask, g2m_src, g2m_dst, live,
            0, 2, g_pre, g_pick, g_scat, acc_g, False,
        )

    @pl.when(has_far)
    def _():
        g_copies["far"].wait_recv()
        g_copies["far_e"].start()
        g_copies["far_w"].start()

    g_copies["e", 1].wait_recv()
    g_copies["twin_e"].start()
    g_copies["w", 1].wait_recv()
    g_copies["twin_w"].start()

    loaded("s3", "e1")
    centre(3)

    def embed_mesh(n):
        embed(
            n * GROUP, GROUP, mesh_efeat, mesh_rows, mesh_mask, mesh_src, mesh_dst, None,
            1, 3, m_pre, m_pick, m_scat, acc_e, True,
        )

    @pl.loop(0, EARLY)
    def _(n):
        embed_mesh(n)

    loaded("s4", "s6", "s5", "s7", "n1")
    for k in (4, 6, 5, 7):
        centre(k)

    for name in (("e", 0), ("w", 0), "twin", "twin_e", "twin_w"):
        g_copies[name].wait_recv()

    @pl.when(has_far)
    def _():
        g_copies["far_e"].wait_recv()
        g_copies["far_w"].wait_recv()

    @pl.loop(0, 6 // GGROUP)
    def _(n):
        update(n * GGROUP, GGROUP, g2m_src, g2m_dst, 4, g_pre, g_pick, g_scat, gt, acc_h)

    def m_at(r, c, b):
        return mt.at[(r * 3 + c) * 3 + b]

    m_on, m_off = 2 * (1 - par), 2 * par
    m_copies = {}
    for b in range(3):
        m_copies["e", b] = remote(("me", b), m_at(1, 1, b), m_at(1, 0, b), east)
        m_copies["w", b] = remote(("mw", b), m_at(1, 1, b), m_at(1, 2, b), west)
        m_copies["far", b] = remote(("mfar", b), m_at(1, 1, b), m_at(m_on, 1, b), far)
        m_copies["twin", b] = remote(("mtwin", b), m_at(1, 1, b), m_at(m_off, 1, b), twin)
        m_copies["far_e", b] = remote(("mfe", b), m_at(m_off, 1, b), m_at(m_off, 0, b), east)
        m_copies["far_w", b] = remote(("mfw", b), m_at(m_off, 1, b), m_at(m_off, 2, b), west)
        m_copies["twin_e", b] = remote(("mte", b), m_at(1, 0, b), m_at(m_off, 0, b), twin)
        m_copies["twin_w", b] = remote(("mtw", b), m_at(1, 2, b), m_at(m_off, 2, b), twin)

    half = pl.ds(pl.multiple_of(par * 256, 256), 256)
    unit = mt.at[NEAR + chip, pl.ds(pl.multiple_of(lon * 16, 16), 16), half]
    c_lon = [remote(("cl", t), unit, unit, mate) for t, mate in enumerate(lon_mates)]
    line = mt.at[NEAR + chip, :, half]
    c_x = remote("cx", line, line, x_mate)
    plane = mt.at[pl.ds(NEAR + 2 * (chip // 2), 2), :, half]
    c_z = [remote(("cz", t), plane, plane, mate) for t, mate in enumerate(z_mates)]
    cube = mt.at[pl.ds(NEAR, 8), :, half]
    c_core = remote("cc", cube, cube, twin)

    g2m_round = (acc_g[...] + acc_h[...] * gain(4)).astype(BF)
    node_w = nf_v[0, 512:1024]
    for b in range(3):
        rows = slice(b * BLK, (b + 1) * BLK)
        u = npre[rows] + mm(g2m_round[rows], node_w)
        step = unit_rows(mm(silu(u), sec_v[6])) * gain(6)
        one = (start_v[rows].astype(F32) + step).astype(BF)
        one_v[rows] = one
        mt[12 + b] = mm(one, ef_v[1, 512:1024]).astype(BF)

        @pl.when(has_far)
        def _(b=b):
            m_copies["far", b].start()

        for name in ("e", "w", "twin"):
            m_copies[name, b].start()

    one = one_v[...]
    dproj[...] = mm(one, ef_v[1, 1024:1536]).astype(BF).reshape(3, BLK, 512)
    m_copies["twin", 0].wait_recv()
    mine = mt[12, 0:16].astype(F32)[0:COARSE]
    other = mt[(m_on * 3 + 1) * 3, 0:16].astype(F32)[0:COARSE]
    top = jnp.where(par == 0, mine, other)
    low = jnp.where(par == 0, other, mine)
    both = jnp.concatenate([top, low], axis=0)
    unit[...] = jnp.where(par == 0, both[:, 0:256], both[:, 256:512]).astype(BF)
    for copy in c_lon:
        copy.start()
    npre[...] = mm(one, nf_v[1, 0:512])

    def forward(b):
        @pl.when(has_far)
        def _():
            m_copies["far", b].wait_recv()
            m_copies["far_e", b].start()
            m_copies["far_w", b].start()

        m_copies["e", b].wait_recv()
        m_copies["twin_e", b].start()
        m_copies["w", b].wait_recv()
        m_copies["twin_w", b].start()

    groups = 24 // GROUP
    late = groups - EARLY

    @pl.loop(EARLY, EARLY + late // 4)
    def _(n):
        embed_mesh(n)

    for copy in c_lon:
        copy.wait_recv()
    c_x.start()
    forward(0)

    @pl.loop(EARLY + late // 4, EARLY + late // 2)
    def _(n):
        embed_mesh(n)

    c_x.wait_recv()
    for copy in c_z:
        copy.start()
    forward(1)

    @pl.loop(EARLY + late // 2, groups)
    def _(n):
        embed_mesh(n)

    forward(2)
    for copy in c_z:
        copy.wait_recv()
    c_core.start()
    for b in range(3):
        if b:
            m_copies["twin", b].wait_recv()
        m_copies["twin_e", b].wait_recv()
        m_copies["twin_w", b].wait_recv()

        @pl.when(has_far)
        def _(b=b):
            m_copies["far_e", b].wait_recv()
            m_copies["far_w", b].wait_recv()

    c_core.wait_recv()

    @pl.loop(0, groups)
    def _(n):
        update(n * GROUP, GROUP, mesh_src, mesh_dst, 5, m_pre, m_pick, m_scat, mt, acc_m)

    mesh_round = (acc_e[...] + acc_m[...] * gain(5)).astype(BF)
    u = npre[...] + mm(mesh_round, nf_v[1, 512:1024])
    step = unit_rows(mm(silu(u), sec_v[7])) * gain(7)
    out[0, 0] = (one_v[...].astype(F32) + step).astype(BF)

    for name, copy in list(g_copies.items()) + list(m_copies.items()):
        kind = name if isinstance(name, str) else name[0]
        if kind.startswith("far"):
            pl.when(has_far)(copy.wait_send)
        else:
            copy.wait_send()
    for copy in c_lon + [c_x] + c_z + [c_core]:
        copy.wait_send()


def per_device(
    grid_feat,
    mesh_feat,
    g2m_feat,
    g2m_src,
    g2m_dst,
    g2m_rows,
    g2m_mask,
    g2m_live,
    mesh_efeat,
    mesh_src,
    mesh_dst,
    mesh_rows,
    mesh_mask,
    grid_in,
    mesh_in,
    edge_in,
    edge_first,
    node_first,
    second,
    norm_gains,
):
    hbm = pl.BlockSpec(memory_space=pl.ANY)
    vmem = pl.BlockSpec(memory_space=pltpu.VMEM)
    smem = pl.BlockSpec(memory_space=pltpu.SMEM)
    copies = 96
    return pl.pallas_call(
        kernel,
        out_shape=jax.ShapeDtypeStruct((1, 1, 384, 512), BF),
        in_specs=[hbm] * 5 + [vmem] * 10 + [smem] * 5,
        out_specs=vmem,
        scratch_shapes=[
            pltpu.VMEM((2, 2, BLK, 474), BF),
            pltpu.VMEM((474, 512), BF),
            pltpu.VMEM((8, 512, 512), BF),
            pltpu.VMEM((2, 1536, 512), BF),
            pltpu.VMEM((2, 1024, 512), BF),
            pltpu.VMEM((16, BLK, 512), BF),
            pltpu.VMEM((NEAR + 8, BLK, 512), BF),
            pltpu.VMEM((384, 512), BF),
            pltpu.VMEM((384, 512), BF),
            pltpu.VMEM((3, BLK, 512), BF),
            pltpu.VMEM((384, 512), F32),
            pltpu.VMEM((6, BLK, 512), F32),
            pltpu.VMEM((6, BLK, 256), BF),
            pltpu.VMEM((6, 384, BLK), BF),
            pltpu.VMEM((24, BLK, 512), F32),
            pltpu.VMEM((24, BLK, 256), BF),
            pltpu.VMEM((24, 384, BLK), BF),
            pltpu.VMEM((384, 512), F32),
            pltpu.VMEM((384, 512), F32),
            pltpu.VMEM((384, 512), F32),
            pltpu.VMEM((384, 512), F32),
            pltpu.SemaphoreType.DMA((14,)),
            pltpu.SemaphoreType.DMA((copies,)),
            pltpu.SemaphoreType.DMA((copies,)),
        ],
        compiler_params=pltpu.CompilerParams(
            collective_id=0, has_side_effects=True, vmem_limit_bytes=56 * 1024 * 1024
        ),
        cost_estimate=pl.CostEstimate(flops=13 * 10**9, bytes_accessed=12 * 2**20, transcendentals=0),
    )(
        grid_feat,
        grid_in,
        second,
        edge_first,
        node_first,
        mesh_feat,
        g2m_feat,
        g2m_rows,
        g2m_mask,
        mesh_efeat,
        mesh_rows,
        mesh_mask,
        mesh_in,
        edge_in,
        norm_gains,
        g2m_src,
        g2m_dst,
        g2m_live,
        mesh_src,
        mesh_dst,
    )


def solution(mesh):
    tile = lambda rank: P("lat", "lon", *([None] * (rank - 2)))
    in_specs = tuple(tile(r) for r in (4, 4, 5, 3, 3, 5, 4, 2, 5, 3, 3, 5, 4)) + (P(),) * 7
    return jax.shard_map(
        per_device, mesh=mesh, in_specs=in_specs, out_specs=tile(4), check_vma=False
    )
```

```python
import functools

import jax
import jax.numpy as jnp
from jax import lax
from jax.experimental import pallas as pl
from jax.experimental.pallas import tpu as pltpu
from jax.sharding import PartitionSpec as P

BF = jnp.bfloat16
F32 = jnp.float32
MESH = pl.DeviceIdType.MESH
BLK = 128
GROUP = 4
UGROUP = 8
GGROUP = 6
EARLY = 2
NEAR = 27
COARSE = 8


def mm(a, b):
    return jnp.dot(a, b, preferred_element_type=F32)


def silu(x):
    half = 0.5 * x
    return (half * jnp.tanh(half) + half).astype(BF)


def unit_rows(v):
    return v * lax.rsqrt(jnp.mean(v * v, axis=-1, keepdims=True) + 1e-05)


def kernel(
    grid_feat,
    grid_in,
    second,
    edge_first,
    node_first,
    mesh_feat_h,
    g2m_feat_h,
    g2m_rows_h,
    g2m_mask_h,
    mesh_efeat_h,
    mesh_rows_h,
    mesh_mask_h,
    mesh_in_h,
    edge_in_h,
    norm_gains_h,
    g2m_src_h,
    g2m_dst_h,
    g2m_live_h,
    mesh_src_h,
    mesh_dst_h,
    out,
    mesh_feat,
    g2m_feat,
    g2m_rows,
    g2m_mask,
    mesh_efeat,
    mesh_rows,
    mesh_mask,
    mesh_in,
    edge_in,
    norm_gains,
    g2m_src,
    g2m_dst,
    g2m_live,
    mesh_src,
    mesh_dst,
    feat_v,
    gin_v,
    sec_v,
    ef_v,
    nf_v,
    gt,
    mt,
    start_v,
    one_v,
    dproj,
    npre,
    g_pre,
    g_pick,
    g_scat,
    m_pre,
    m_pick,
    m_scat,
    acc_e,
    acc_m,
    acc_g,
    acc_h,
    load_sem,
    send_sem,
    recv_sem,
):
    lat, lon = lax.axis_index("lat"), lax.axis_index("lon")
    n_lat, n_lon = lax.axis_size("lat"), lax.axis_size("lon")
    par = lax.rem(lat, 2)
    chip = lat // 2
    east = (lat, lax.rem(lon + 1, n_lon))
    west = (lat, lax.rem(lon + n_lon - 1, n_lon))
    twin = (lat + 1 - 2 * par, lon)
    far_lat = lat + 2 * par - 1
    has_far = jnp.logical_and(far_lat >= 0, far_lat < n_lat)
    far = (far_lat, lon)
    y = lax.rem(lon, 4)
    diag_e, diag_w = (far_lat, east[1]), (far_lat, west[1])
    is_y = [jnp.logical_and(has_far, y == k) for k in range(4)]
    inner = jnp.logical_and(has_far, jnp.logical_or(y == 1, y == 2))
    outer = jnp.logical_and(has_far, jnp.logical_or(y == 0, y == 3))
    x_lat = lat + 2 - 4 * lax.rem(chip, 2)
    plane_mates = [(lat, lax.rem(lon + t, n_lon)) for t in range(1, n_lon)]
    plane_mates += [(x_lat, lax.rem(lon + t, n_lon)) for t in range(n_lon)]
    z_mates = [(lax.rem(lat + 4 * t, n_lat), lon) for t in range(1, n_lat // 4)]

    loads = {}

    def load(name, src, dst):
        copy = pltpu.make_async_copy(src, dst, load_sem.at[len(loads)])
        copy.start()
        loads[name] = copy

    def loaded(*names):
        for name in names:
            loads[name].wait()

    load("feat", grid_feat, feat_v)
    load("gin", grid_in, gin_v)
    load("s0", second.at[0], sec_v.at[0])
    load("gains", norm_gains_h, norm_gains)
    load("e0", edge_first.at[0], ef_v.at[0])
    load("mesh_feat", mesh_feat_h, mesh_feat)
    load("mesh_in", mesh_in_h, mesh_in)
    load("s1", second.at[1], sec_v.at[1])
    load("s2", second.at[2], sec_v.at[2])
    load("edge_in", edge_in_h, edge_in)
    for name, source, target in (
        ("g2m_feat", g2m_feat_h, g2m_feat),
        ("g2m_rows", g2m_rows_h, g2m_rows),
        ("g2m_mask", g2m_mask_h, g2m_mask),
        ("g2m_src", g2m_src_h, g2m_src),
        ("g2m_dst", g2m_dst_h, g2m_dst),
        ("g2m_live", g2m_live_h, g2m_live),
    ):
        load(name, source, target)
    load("n0", node_first.at[0], nf_v.at[0])
    for name, source, target in (
        ("mesh_efeat", mesh_efeat_h, mesh_efeat),
        ("mesh_rows", mesh_rows_h, mesh_rows),
        ("mesh_mask", mesh_mask_h, mesh_mask),
        ("mesh_src", mesh_src_h, mesh_src),
        ("mesh_dst", mesh_dst_h, mesh_dst),
    ):
        load(name, source, target)
    load("s3", second.at[3], sec_v.at[3])
    load("e1", edge_first.at[1], ef_v.at[1])
    load("s4", second.at[4], sec_v.at[4])
    load("s6", second.at[6], sec_v.at[6])
    load("s5", second.at[5], sec_v.at[5])
    load("n1", node_first.at[1], nf_v.at[1])
    load("s7", second.at[7], sec_v.at[7])

    barrier = pltpu.get_barrier_semaphore()
    mates = plane_mates + [twin] + z_mates
    for mate in mates:
        pl.semaphore_signal(barrier, inc=1, device_id=mate, device_id_type=MESH)

    @pl.when(has_far)
    def _():
        pl.semaphore_signal(barrier, inc=1, device_id=far, device_id_type=MESH)

    for needed, diag in ((is_y[3], diag_e), (is_y[0], diag_w)):

        @pl.when(needed)
        def _(diag=diag):
            pl.semaphore_signal(barrier, inc=1, device_id=diag, device_id_type=MESH)

    peers = jnp.where(has_far, 1, 0) + jnp.where(outer, 1, 0)
    def gain(k):
        return norm_gains[...].astype(F32)[k : k + 1]

    def centre(k):
        w = sec_v[k].astype(F32)
        sec_v[k] = (w - jnp.mean(w, axis=-1, keepdims=True)).astype(BF)

    numbers = {}

    def remote(name, src, dst, device, sender=None):
        index = numbers.setdefault(name, len(numbers))
        leave = numbers.setdefault(sender or name, len(numbers))
        return pltpu.make_async_remote_copy(
            src_ref=src,
            dst_ref=dst,
            send_sem=send_sem.at[leave],
            recv_sem=recv_sem.at[index],
            device_id=device,
            device_id_type=MESH,
        )

    def g_at(r, c, n=1):
        return gt.at[pl.ds(r * 4 + c, n)]

    on_row, off_row = 3 * (1 - par), 3 * par
    g_rows = (1 + par, 2 - par)
    g_copies = {}
    for t in range(2):
        g_copies["e", t] = remote(("ge", t), g_at(g_rows[t], 2), g_at(g_rows[t], 0), east)
        g_copies["w", t] = remote(("gw", t), g_at(g_rows[t], 1), g_at(g_rows[t], 3), west)
    g_copies["far"] = remote("gfar", g_at(g_rows[0], 1, 2), g_at(on_row, 1, 2), far)
    g_copies["twin"] = remote("gtwin", g_at(g_rows[1], 1, 2), g_at(off_row, 1, 2), twin)
    g_copies["far_e"] = remote("gfe", g_at(off_row, 2), g_at(off_row, 0), east)
    g_copies["far_w"] = remote("gfw", g_at(off_row, 1), g_at(off_row, 3), west)
    g_diag_e = remote("gfe", g_at(g_rows[0], 2), g_at(on_row, 0), diag_e, "gdiag")
    g_side_w = remote("gfe", g_at(g_rows[0], 0), g_at(on_row, 0), far, "gside")
    g_side_e = remote("gfw", g_at(g_rows[0], 3), g_at(on_row, 3), far, "gside")
    g_diag_w = remote("gfw", g_at(g_rows[0], 1), g_at(on_row, 3), diag_w, "gdiag")
    g_copies["twin_e"] = remote("gte", g_at(g_rows[1], 0), g_at(off_row, 0), twin)
    g_copies["twin_w"] = remote("gtw", g_at(g_rows[1], 3), g_at(off_row, 3), twin)

    @pl.when(jnp.logical_not(has_far))
    def _():
        gt[pl.ds(off_row * 4, 4)] = jnp.zeros((4, BLK, 512), BF)
        mt[pl.ds(2 * par * 9, 9)] = jnp.zeros((9, BLK, 512), BF)

    loaded("feat", "gin", "s0", "gains")
    centre(0)
    w_in = gin_v[...]
    for t in range(2):
        x = feat_v[g_rows[t] - 1].reshape(2 * BLK, -1)
        v = mm(silu(mm(x, w_in)), sec_v[0])
        latent = (unit_rows(v) * gain(0)).astype(BF)
        if t == 0:
            loaded("e0")
        proj = mm(latent, ef_v[0, 512:1024]).astype(BF)
        gt[pl.ds(g_rows[t] * 4 + 1, 2)] = proj.reshape(2, BLK, 512)
        if t == 0:
            pl.semaphore_wait(barrier, len(mates) + peers)

            @pl.when(has_far)
            def _():
                g_copies["far"].start()

            pl.when(is_y[3])(g_diag_e.start)
            pl.when(is_y[0])(g_diag_w.start)

        else:
            g_copies["twin"].start()
        g_copies["e", t].start()
        g_copies["w", t].start()

    loaded("s1", "mesh_feat", "mesh_in")
    centre(1)
    u = lax.dot_general(
        mesh_feat[0, 0], mesh_in[...], (((0,), (0,)), ((), ())), preferred_element_type=F32
    )
    start = (unit_rows(mm(silu(u), sec_v[1])) * gain(1)).astype(BF)
    start_v[...] = start
    dproj[...] = mm(start, ef_v[0, 1024:1536]).astype(BF).reshape(3, BLK, 512)
    loaded("n0")
    npre[...] = mm(start, nf_v[0, 0:512])

    def embed(base, count, feat, rows, mask, src, dst, live, layer, k, pre, pick, scat, acc, far_blocks):
        w_edge = edge_in[layer]
        hidden = []
        scatters = []
        spot = lax.broadcasted_iota(jnp.int32, (BLK, BLK), 0)
        place = lax.broadcasted_iota(jnp.int32, (3 * BLK, BLK), 0)
        for q in range(count):
            s = base + q
            u = lax.dot_general(
                feat[0, 0, s], w_edge, (((0,), (0,)), ((), ())), preferred_element_type=F32
            )
            hidden.append(silu(u))
            pair = rows[0, 0, s]
            hs, hd = pair[0:1], pair[1:2]
            if far_blocks:
                moved = ((hs >> 3) & 7) * 16 + (hs >> 6) * 8 + (hs & 7)
                is_coarse = jnp.where(src[0, 0, s] >= NEAR, 1, 0)
                hs = hs + is_coarse * (moved - hs)
            pick_s = jnp.where(spot == hs, 1.0, 0.0).T.astype(BF)
            pick_d = jnp.where(spot == hd, 1.0, 0.0).T.astype(BF)
            pick[s] = jnp.concatenate([pick_s, pick_d], axis=1)
            if live is None:
                keep = mask[0, 0, pl.ds(s, 1), :]
            else:
                keep = mask[0, s] * jnp.where(s < live, 1, 0)
            target = jnp.where(keep != 0, hd + BLK * dst[0, 0, s], -1)
            one = jnp.where(place == target, 1.0, 0.0).astype(BF)
            scat[s] = one
            scatters.append(one)
        e = (unit_rows(mm(jnp.concatenate(hidden, axis=0), sec_v[k])) * gain(k)).astype(BF)
        pre[pl.ds(base, count)] = mm(e, ef_v[layer, 0:512]).reshape(count, BLK, 512)
        acc[...] += mm(jnp.concatenate(scatters, axis=1), e)

    def update(base, count, src, dst, k, pre, pick, scat, table, acc):
        hidden = []
        for q in range(count):
            s = base + q
            blocks = jnp.concatenate([table[src[0, 0, s]], dproj[dst[0, 0, s]]], axis=0)
            hidden.append(silu(pre[s] + mm(pick[s], blocks)))
        message = unit_rows(mm(jnp.concatenate(hidden, axis=0), sec_v[k])).astype(BF)
        scatters = jnp.concatenate([scat[base + q] for q in range(count)], axis=1)
        acc[...] += mm(scatters, message)

    zeros = jnp.zeros(acc_e.shape, F32)
    acc_e[...] = zeros
    acc_m[...] = zeros
    acc_g[...] = zeros
    acc_h[...] = zeros
    loaded("s2", "edge_in", "g2m_feat", "g2m_rows", "g2m_mask", "g2m_src", "g2m_dst", "g2m_live")
    live = g2m_live[0, 0]
    centre(2)

    @pl.loop(0, 6 // GGROUP)
    def _(n):
        embed(
            n * GGROUP, GGROUP, g2m_feat, g2m_rows, g2m_mask, g2m_src, g2m_dst, live,
            0, 2, g_pre, g_pick, g_scat, acc_g, False,
        )

    pl.when(has_far)(g_copies["far"].wait_recv)
    pl.when(inner)(g_copies["far_e"].start)
    pl.when(inner)(g_copies["far_w"].start)
    pl.when(y == 1)(g_copies["e", 0].wait_recv)
    pl.when(is_y[1])(g_side_w.start)
    pl.when(y == 2)(g_copies["w", 0].wait_recv)
    pl.when(is_y[2])(g_side_e.start)

    loaded("s3", "e1", "mesh_efeat", "mesh_rows", "mesh_mask", "mesh_src", "mesh_dst")
    centre(3)

    def embed_mesh(n):
        embed(
            n * GROUP, GROUP, mesh_efeat, mesh_rows, mesh_mask, mesh_src, mesh_dst, None,
            1, 3, m_pre, m_pick, m_scat, acc_e, True,
        )

    @pl.loop(0, EARLY)
    def _(n):
        embed_mesh(n)

    loaded("s4", "s6", "s5", "s7", "n1")
    for k in (4, 6, 5, 7):
        centre(k)

    g_copies["e", 1].wait_recv()
    g_copies["twin_e"].start()
    g_copies["w", 1].wait_recv()
    g_copies["twin_w"].start()
    pl.when(y != 1)(g_copies["e", 0].wait_recv)
    pl.when(y != 2)(g_copies["w", 0].wait_recv)
    for name in ("twin", "twin_e", "twin_w"):
        g_copies[name].wait_recv()

    @pl.when(has_far)
    def _():
        g_copies["far_e"].wait_recv()
        g_copies["far_w"].wait_recv()

    @pl.loop(0, 6 // GGROUP)
    def _(n):
        update(n * GGROUP, GGROUP, g2m_src, g2m_dst, 4, g_pre, g_pick, g_scat, gt, acc_h)

    def m_at(r, c, b):
        return mt.at[(r * 3 + c) * 3 + b]

    m_on, m_off = 2 * (1 - par), 2 * par
    m_copies = {}
    for b in range(3):
        m_copies["e", b] = remote(("me", b), m_at(1, 1, b), m_at(1, 0, b), east)
        m_copies["w", b] = remote(("mw", b), m_at(1, 1, b), m_at(1, 2, b), west)
        m_copies["far", b] = remote(("mfar", b), m_at(1, 1, b), m_at(m_on, 1, b), far)
        m_copies["twin", b] = remote(("mtwin", b), m_at(1, 1, b), m_at(m_off, 1, b), twin)
        m_copies["far_e", b] = remote(("mfe", b), m_at(m_off, 1, b), m_at(m_off, 0, b), east)
        m_copies["far_w", b] = remote(("mfw", b), m_at(m_off, 1, b), m_at(m_off, 2, b), west)
        m_copies["twin_e", b] = remote(("mte", b), m_at(1, 0, b), m_at(m_off, 0, b), twin)
        m_copies["twin_w", b] = remote(("mtw", b), m_at(1, 2, b), m_at(m_off, 2, b), twin)

    m_diag_e = [remote(("mfe", b), m_at(1, 1, b), m_at(m_on, 0, b), diag_e, ("md", b)) for b in range(3)]
    m_side_w = [remote(("mfe", b), m_at(1, 0, b), m_at(m_on, 0, b), far, ("ms", b)) for b in range(3)]
    m_side_e = [remote(("mfw", b), m_at(1, 2, b), m_at(m_on, 2, b), far, ("ms", b)) for b in range(3)]
    m_diag_w = [remote(("mfw", b), m_at(1, 1, b), m_at(m_on, 2, b), diag_w, ("md", b)) for b in range(3)]

    half = pl.ds(pl.multiple_of(par * 256, 256), 256)
    unit = mt.at[NEAR + chip, pl.ds(pl.multiple_of(lon * 16, 16), 16), half]
    c_unit = [remote(("cu", t), unit, unit, mate) for t, mate in enumerate(plane_mates)]
    z = chip // 2

    def plane(t):
        return mt.at[pl.ds(NEAR + 2 * lax.rem(z + t, 4), 2), :, half]

    c_z = [remote(("cz", t), plane(0), plane(0), mate) for t, mate in enumerate(z_mates)]
    c_twin = [remote(("cc", t), plane(t), plane(t), twin) for t in range(4)]

    def coarse_out():
        m_copies["twin", 0].wait_recv()
        mine = mt[12, 0:16].astype(F32)[0:COARSE]
        other = mt[(m_on * 3 + 1) * 3, 0:16].astype(F32)[0:COARSE]
        top = jnp.where(par == 0, mine, other)
        low = jnp.where(par == 0, other, mine)
        both = jnp.concatenate([top, low], axis=0)
        unit[...] = jnp.where(par == 0, both[:, 0:256], both[:, 256:512]).astype(BF)
        for copy in c_unit:
            copy.start()

    def patch_out(b):
        pl.when(has_far)(m_copies["far", b].start)
        pl.when(is_y[3])(m_diag_e[b].start)
        pl.when(is_y[0])(m_diag_w[b].start)
        m_copies["e", b].start()
        m_copies["w", b].start()

    g2m_round = (acc_g[...] + acc_h[...] * gain(4)).astype(BF)
    node_w = nf_v[0, 512:1024]
    for b in range(3):
        rows = slice(b * BLK, (b + 1) * BLK)
        u = npre[rows] + mm(g2m_round[rows], node_w)
        step = unit_rows(mm(silu(u), sec_v[6])) * gain(6)
        one = (start_v[rows].astype(F32) + step).astype(BF)
        one_v[rows] = one
        mt[12 + b] = mm(one, ef_v[1, 512:1024]).astype(BF)

        m_copies["twin", b].start()
        if b == 1:
            coarse_out()
            patch_out(0)
        if b >= 1:
            patch_out(b)

    one = one_v[...]
    dproj[...] = mm(one, ef_v[1, 1024:1536]).astype(BF).reshape(3, BLK, 512)
    npre[...] = mm(one, nf_v[1, 0:512])

    def corners(b):
        pl.when(has_far)(m_copies["far", b].wait_recv)
        pl.when(inner)(m_copies["far_e", b].start)
        pl.when(inner)(m_copies["far_w", b].start)
        pl.when(y == 1)(m_copies["e", b].wait_recv)
        pl.when(is_y[1])(m_side_w[b].start)
        pl.when(y == 2)(m_copies["w", b].wait_recv)
        pl.when(is_y[2])(m_side_e[b].start)

    groups = 24 // GROUP

    pl.loop(EARLY, EARLY + 2)(embed_mesh)
    for copy in c_unit:
        copy.wait_recv()
    for t in (0, 2, 1):
        c_z[t].start()
    c_twin[0].start()
    pl.when(inner)(functools.partial(corners, 0))
    pl.loop(EARLY + 2, EARLY + 3)(embed_mesh)
    pl.when(inner)(functools.partial(corners, 1))
    pl.loop(EARLY + 3, groups)(embed_mesh)
    pl.when(inner)(functools.partial(corners, 2))
    for t in (0, 2, 1):
        c_z[t].wait_recv()
        c_twin[3 - t].start()
    for b in range(3):
        @pl.when(jnp.logical_not(inner))
        def _(b=b):
            corners(b)

        if b:
            m_copies["twin", b].wait_recv()
        pl.when(y != 1)(m_copies["e", b].wait_recv)
        m_copies["twin_e", b].start()
        pl.when(y != 2)(m_copies["w", b].wait_recv)
        m_copies["twin_w", b].start()
    for b in range(3):
        m_copies["twin_e", b].wait_recv()
        m_copies["twin_w", b].wait_recv()
        pl.when(has_far)(m_copies["far_e", b].wait_recv)
        pl.when(has_far)(m_copies["far_w", b].wait_recv)
    for copy in c_twin:
        copy.wait_recv()

    @pl.loop(0, 24 // UGROUP)
    def _(n):
        update(n * UGROUP, UGROUP, mesh_src, mesh_dst, 5, m_pre, m_pick, m_scat, mt, acc_m)

    mesh_round = (acc_e[...] + acc_m[...] * gain(5)).astype(BF)
    u = npre[...] + mm(mesh_round, nf_v[1, 512:1024])
    step = unit_rows(mm(silu(u), sec_v[7])) * gain(7)
    out[0, 0] = (one_v[...].astype(F32) + step).astype(BF)

    pl.when(outer)(g_diag_e.wait_send)
    pl.when(inner)(g_side_e.wait_send)
    for b in range(3):
        pl.when(outer)(m_diag_e[b].wait_send)
        pl.when(inner)(m_side_e[b].wait_send)
    for name, copy in list(g_copies.items()) + list(m_copies.items()):
        kind = name if isinstance(name, str) else name[0]
        if kind == "far":
            pl.when(has_far)(copy.wait_send)
        elif kind.startswith("far"):
            pl.when(inner)(copy.wait_send)
        else:
            copy.wait_send()
    for copy in c_unit + c_z + c_twin:
        copy.wait_send()


def per_device(
    grid_feat,
    mesh_feat,
    g2m_feat,
    g2m_src,
    g2m_dst,
    g2m_rows,
    g2m_mask,
    g2m_live,
    mesh_efeat,
    mesh_src,
    mesh_dst,
    mesh_rows,
    mesh_mask,
    grid_in,
    mesh_in,
    edge_in,
    edge_first,
    node_first,
    second,
    norm_gains,
):
    hbm = pl.BlockSpec(memory_space=pl.ANY)
    vmem = pl.BlockSpec(memory_space=pltpu.VMEM)
    g2m_mask = jnp.swapaxes(g2m_mask, 1, 2)
    small = (
        mesh_feat,
        g2m_feat,
        g2m_rows,
        g2m_mask,
        mesh_efeat,
        mesh_rows,
        mesh_mask,
        mesh_in,
        edge_in,
        norm_gains,
    )
    scalars = (g2m_src, g2m_dst, g2m_live, mesh_src, mesh_dst)
    copies = 96
    return pl.pallas_call(
        kernel,
        out_shape=jax.ShapeDtypeStruct((1, 1, 384, 512), BF),
        in_specs=[hbm] * 20,
        out_specs=vmem,
        scratch_shapes=[pltpu.VMEM(x.shape, x.dtype) for x in small]
        + [pltpu.SMEM(x.shape, x.dtype) for x in scalars]
        + [
            pltpu.VMEM((2, 2, BLK, 474), BF),
            pltpu.VMEM((474, 512), BF),
            pltpu.VMEM((8, 512, 512), BF),
            pltpu.VMEM((2, 1536, 512), BF),
            pltpu.VMEM((2, 1024, 512), BF),
            pltpu.VMEM((16, BLK, 512), BF),
            pltpu.VMEM((NEAR + 8, BLK, 512), BF),
            pltpu.VMEM((384, 512), BF),
            pltpu.VMEM((384, 512), BF),
            pltpu.VMEM((3, BLK, 512), BF),
            pltpu.VMEM((384, 512), F32),
            pltpu.VMEM((6, BLK, 512), F32),
            pltpu.VMEM((6, BLK, 256), BF),
            pltpu.VMEM((6, 384, BLK), BF),
            pltpu.VMEM((24, BLK, 512), F32),
            pltpu.VMEM((24, BLK, 256), BF),
            pltpu.VMEM((24, 384, BLK), BF),
            pltpu.VMEM((384, 512), F32),
            pltpu.VMEM((384, 512), F32),
            pltpu.VMEM((384, 512), F32),
            pltpu.VMEM((384, 512), F32),
            pltpu.SemaphoreType.DMA((32,)),
            pltpu.SemaphoreType.DMA((copies,)),
            pltpu.SemaphoreType.DMA((copies,)),
        ],
        compiler_params=pltpu.CompilerParams(
            collective_id=0, has_side_effects=True, vmem_limit_bytes=56 * 1024 * 1024
        ),
        cost_estimate=pl.CostEstimate(flops=13 * 10**9, bytes_accessed=12 * 2**20, transcendentals=0),
    )(
        grid_feat,
        grid_in,
        second,
        edge_first,
        node_first,
        *small,
        *scalars,
    )


def solution(mesh):
    tile = lambda rank: P("lat", "lon", *([None] * (rank - 2)))
    in_specs = tuple(tile(r) for r in (4, 4, 5, 3, 3, 5, 4, 2, 5, 3, 3, 5, 4)) + (P(),) * 7
    return jax.shard_map(
        per_device, mesh=mesh, in_specs=in_specs, out_specs=tile(4), check_vma=False
    )
```

```python
import functools

import jax
import jax.numpy as jnp
from jax import lax
from jax.experimental import pallas as pl
from jax.experimental.pallas import tpu as pltpu
from jax.sharding import PartitionSpec as P

BF = jnp.bfloat16
F32 = jnp.float32
MESH = pl.DeviceIdType.MESH
BLK = 128
GROUP = 4
UGROUP = 12
GGROUP = 6
EARLY = 2
NEAR = 27
COARSE = 8


def mm(a, b):
    return jnp.dot(a, b, preferred_element_type=F32)


def silu(x):
    half = 0.5 * x
    return (half * jnp.tanh(half) + half).astype(BF)


def unit_rows(v):
    return v * lax.rsqrt(jnp.mean(v * v, axis=-1, keepdims=True) + 1e-05)


def kernel(
    grid_feat,
    grid_in,
    second,
    edge_first,
    node_first,
    mesh_feat_h,
    g2m_feat_h,
    g2m_rows_h,
    g2m_mask_h,
    mesh_efeat_h,
    mesh_rows_h,
    mesh_mask_h,
    mesh_in_h,
    edge_in_h,
    norm_gains_h,
    g2m_src_h,
    g2m_dst_h,
    g2m_live_h,
    mesh_src_h,
    mesh_dst_h,
    out,
    mesh_feat,
    g2m_feat,
    g2m_rows,
    g2m_mask,
    mesh_efeat,
    mesh_rows,
    mesh_mask,
    mesh_in,
    edge_in,
    norm_gains,
    g2m_src,
    g2m_dst,
    g2m_live,
    mesh_src,
    mesh_dst,
    feat_v,
    gin_v,
    sec_v,
    ef_v,
    nf_v,
    gt,
    mt,
    start_v,
    one_v,
    dproj,
    npre,
    g_pre,
    g_pick,
    g_scat,
    m_pre,
    m_pick,
    m_scat,
    acc_e,
    acc_m,
    acc_g,
    acc_h,
    load_sem,
    send_sem,
    recv_sem,
):
    lat, lon = lax.axis_index("lat"), lax.axis_index("lon")
    n_lat, n_lon = lax.axis_size("lat"), lax.axis_size("lon")
    par = lax.rem(lat, 2)
    chip = lat // 2
    east = (lat, lax.rem(lon + 1, n_lon))
    west = (lat, lax.rem(lon + n_lon - 1, n_lon))
    twin = (lat + 1 - 2 * par, lon)
    far_lat = lat + 2 * par - 1
    has_far = jnp.logical_and(far_lat >= 0, far_lat < n_lat)
    far = (far_lat, lon)
    y = lax.rem(lon, 4)
    diag_e, diag_w = (far_lat, east[1]), (far_lat, west[1])
    is_y = [jnp.logical_and(has_far, y == k) for k in range(4)]
    inner = jnp.logical_and(has_far, jnp.logical_or(y == 1, y == 2))
    outer = jnp.logical_and(has_far, jnp.logical_or(y == 0, y == 3))
    x_lat = lat + 2 - 4 * lax.rem(chip, 2)
    plane_mates = [(lat, lax.rem(lon + t, n_lon)) for t in range(1, n_lon)]
    plane_mates += [(x_lat, lax.rem(lon + t, n_lon)) for t in range(n_lon)]
    z_mates = [(lax.rem(lat + 4 * t, n_lat), lon) for t in range(1, n_lat // 4)]

    loads = {}

    def load(name, src, dst):
        copy = pltpu.make_async_copy(src, dst, load_sem.at[len(loads)])
        copy.start()
        loads[name] = copy

    def loaded(*names):
        for name in names:
            loads[name].wait()

    load("feat", grid_feat, feat_v)
    load("gin", grid_in, gin_v)
    load("s0", second.at[0], sec_v.at[0])
    load("gains", norm_gains_h, norm_gains)
    load("e0", edge_first.at[0], ef_v.at[0])
    load("mesh_feat", mesh_feat_h, mesh_feat)
    load("mesh_in", mesh_in_h, mesh_in)
    load("s1", second.at[1], sec_v.at[1])
    load("s2", second.at[2], sec_v.at[2])
    load("edge_in", edge_in_h, edge_in)
    for name, source, target in (
        ("g2m_feat", g2m_feat_h, g2m_feat),
        ("g2m_rows", g2m_rows_h, g2m_rows),
        ("g2m_mask", g2m_mask_h, g2m_mask),
        ("g2m_src", g2m_src_h, g2m_src),
        ("g2m_dst", g2m_dst_h, g2m_dst),
        ("g2m_live", g2m_live_h, g2m_live),
    ):
        load(name, source, target)
    load("n0", node_first.at[0], nf_v.at[0])
    for name, source, target in (
        ("mesh_efeat", mesh_efeat_h, mesh_efeat),
        ("mesh_rows", mesh_rows_h, mesh_rows),
        ("mesh_mask", mesh_mask_h, mesh_mask),
        ("mesh_src", mesh_src_h, mesh_src),
        ("mesh_dst", mesh_dst_h, mesh_dst),
    ):
        load(name, source, target)
    load("s3", second.at[3], sec_v.at[3])
    load("e1", edge_first.at[1], ef_v.at[1])
    load("s4", second.at[4], sec_v.at[4])
    load("s6", second.at[6], sec_v.at[6])
    load("s5", second.at[5], sec_v.at[5])
    load("n1", node_first.at[1], nf_v.at[1])
    load("s7", second.at[7], sec_v.at[7])

    barrier = pltpu.get_barrier_semaphore()
    mates = plane_mates + [twin] + z_mates
    for mate in mates:
        pl.semaphore_signal(barrier, inc=1, device_id=mate, device_id_type=MESH)

    @pl.when(has_far)
    def _():
        pl.semaphore_signal(barrier, inc=1, device_id=far, device_id_type=MESH)

    for needed, diag in ((is_y[3], diag_e), (is_y[0], diag_w)):

        @pl.when(needed)
        def _(diag=diag):
            pl.semaphore_signal(barrier, inc=1, device_id=diag, device_id_type=MESH)

    peers = jnp.where(has_far, 1, 0) + jnp.where(outer, 1, 0)
    def gain(k):
        return norm_gains[...].astype(F32)[k : k + 1]

    def centre(k):
        w = sec_v[k].astype(F32)
        sec_v[k] = (w - jnp.mean(w, axis=-1, keepdims=True)).astype(BF)

    numbers = {}

    def remote(name, src, dst, device, sender=None):
        index = numbers.setdefault(name, len(numbers))
        leave = numbers.setdefault(sender or name, len(numbers))
        return pltpu.make_async_remote_copy(
            src_ref=src,
            dst_ref=dst,
            send_sem=send_sem.at[leave],
            recv_sem=recv_sem.at[index],
            device_id=device,
            device_id_type=MESH,
        )

    def g_at(r, c, n=1):
        return gt.at[pl.ds(r * 4 + c, n)]

    on_row, off_row = 3 * (1 - par), 3 * par
    g_rows = (1 + par, 2 - par)
    g_copies = {}
    for t in range(2):
        g_copies["e", t] = remote(("ge", t), g_at(g_rows[t], 2), g_at(g_rows[t], 0), east)
        g_copies["w", t] = remote(("gw", t), g_at(g_rows[t], 1), g_at(g_rows[t], 3), west)
    g_copies["far"] = remote("gfar", g_at(g_rows[0], 1, 2), g_at(on_row, 1, 2), far)
    g_copies["twin"] = remote("gtwin", g_at(g_rows[1], 1, 2), g_at(off_row, 1, 2), twin)
    g_copies["far_e"] = remote("gfe", g_at(off_row, 2), g_at(off_row, 0), east)
    g_copies["far_w"] = remote("gfw", g_at(off_row, 1), g_at(off_row, 3), west)
    g_diag_e = remote("gfe", g_at(g_rows[0], 2), g_at(on_row, 0), diag_e, "gdiag")
    g_side_w = remote("gfe", g_at(g_rows[0], 0), g_at(on_row, 0), far, "gside")
    g_side_e = remote("gfw", g_at(g_rows[0], 3), g_at(on_row, 3), far, "gside")
    g_diag_w = remote("gfw", g_at(g_rows[0], 1), g_at(on_row, 3), diag_w, "gdiag")
    g_copies["twin_e"] = remote("gte", g_at(g_rows[1], 0), g_at(off_row, 0), twin)
    g_copies["twin_w"] = remote("gtw", g_at(g_rows[1], 3), g_at(off_row, 3), twin)

    @pl.when(jnp.logical_not(has_far))
    def _():
        gt[pl.ds(off_row * 4, 4)] = jnp.zeros((4, BLK, 512), BF)
        mt[pl.ds(2 * par * 9, 9)] = jnp.zeros((9, BLK, 512), BF)

    loaded("feat", "gin", "s0", "gains")
    centre(0)
    w_in = gin_v[...]
    for t in range(2):
        x = feat_v[g_rows[t] - 1].reshape(2 * BLK, -1)
        v = mm(silu(mm(x, w_in)), sec_v[0])
        latent = (unit_rows(v) * gain(0)).astype(BF)
        if t == 0:
            loaded("e0")
        proj = mm(latent, ef_v[0, 512:1024]).astype(BF)
        gt[pl.ds(g_rows[t] * 4 + 1, 2)] = proj.reshape(2, BLK, 512)
        if t == 0:
            pl.semaphore_wait(barrier, len(mates) + peers)

            @pl.when(has_far)
            def _():
                g_copies["far"].start()

            pl.when(is_y[3])(g_diag_e.start)
            pl.when(is_y[0])(g_diag_w.start)

        else:
            g_copies["twin"].start()
        g_copies["e", t].start()
        g_copies["w", t].start()

    loaded("s1", "mesh_feat", "mesh_in")
    centre(1)
    u = lax.dot_general(
        mesh_feat[0, 0], mesh_in[...], (((0,), (0,)), ((), ())), preferred_element_type=F32
    )
    start = (unit_rows(mm(silu(u), sec_v[1])) * gain(1)).astype(BF)
    start_v[...] = start
    dproj[...] = mm(start, ef_v[0, 1024:1536]).astype(BF).reshape(3, BLK, 512)
    loaded("n0")
    npre[...] = mm(start, nf_v[0, 0:512])

    def embed(base, count, feat, rows, mask, src, dst, live, layer, k, pre, pick, scat, acc, far_blocks):
        w_edge = edge_in[layer]
        hidden = []
        scatters = []
        spot = lax.broadcasted_iota(jnp.int32, (BLK, BLK), 0)
        place = lax.broadcasted_iota(jnp.int32, (3 * BLK, BLK), 0)
        for q in range(count):
            s = base + q
            u = lax.dot_general(
                feat[0, 0, s], w_edge, (((0,), (0,)), ((), ())), preferred_element_type=F32
            )
            hidden.append(silu(u))
            pair = rows[0, 0, s]
            hs, hd = pair[0:1], pair[1:2]
            if far_blocks:
                moved = ((hs >> 3) & 7) * 16 + (hs >> 6) * 8 + (hs & 7)
                is_coarse = jnp.where(src[0, 0, s] >= NEAR, 1, 0)
                hs = hs + is_coarse * (moved - hs)
            pick_s = jnp.where(spot == hs, 1.0, 0.0).T.astype(BF)
            pick_d = jnp.where(spot == hd, 1.0, 0.0).T.astype(BF)
            pick[s] = jnp.concatenate([pick_s, pick_d], axis=1)
            if live is None:
                keep = mask[0, 0, pl.ds(s, 1), :]
            else:
                keep = mask[0, s] * jnp.where(s < live, 1, 0)
            target = jnp.where(keep != 0, hd + BLK * dst[0, 0, s], -1)
            one = jnp.where(place == target, 1.0, 0.0).astype(BF)
            scat[s] = one
            scatters.append(one)
        e = (unit_rows(mm(jnp.concatenate(hidden, axis=0), sec_v[k])) * gain(k)).astype(BF)
        pre[pl.ds(base, count)] = mm(e, ef_v[layer, 0:512]).reshape(count, BLK, 512)
        acc[...] += mm(jnp.concatenate(scatters, axis=1), e)

    def update(base, count, src, dst, k, pre, pick, scat, table, acc):
        hidden = []
        for q in range(count):
            s = base + q
            blocks = jnp.concatenate([table[src[0, 0, s]], dproj[dst[0, 0, s]]], axis=0)
            hidden.append(silu(pre[s] + mm(pick[s], blocks)))
        message = unit_rows(mm(jnp.concatenate(hidden, axis=0), sec_v[k])).astype(BF)
        scatters = jnp.concatenate([scat[base + q] for q in range(count)], axis=1)
        acc[...] += mm(scatters, message)

    zeros = jnp.zeros(acc_e.shape, F32)
    acc_e[...] = zeros
    acc_m[...] = zeros
    acc_g[...] = zeros
    acc_h[...] = zeros
    loaded("s2", "edge_in", "g2m_feat", "g2m_rows", "g2m_mask", "g2m_src", "g2m_dst", "g2m_live")
    live = g2m_live[0, 0]
    centre(2)

    @pl.loop(0, 6 // GGROUP)
    def _(n):
        embed(
            n * GGROUP, GGROUP, g2m_feat, g2m_rows, g2m_mask, g2m_src, g2m_dst, live,
            0, 2, g_pre, g_pick, g_scat, acc_g, False,
        )

    pl.when(has_far)(g_copies["far"].wait_recv)
    pl.when(inner)(g_copies["far_e"].start)
    pl.when(inner)(g_copies["far_w"].start)
    pl.when(y == 1)(g_copies["e", 0].wait_recv)
    pl.when(is_y[1])(g_side_w.start)
    pl.when(y == 2)(g_copies["w", 0].wait_recv)
    pl.when(is_y[2])(g_side_e.start)

    loaded("s3", "e1", "mesh_efeat", "mesh_rows", "mesh_mask", "mesh_src", "mesh_dst")
    centre(3)

    def embed_mesh(n):
        embed(
            n * GROUP, GROUP, mesh_efeat, mesh_rows, mesh_mask, mesh_src, mesh_dst, None,
            1, 3, m_pre, m_pick, m_scat, acc_e, True,
        )

    @pl.loop(0, EARLY)
    def _(n):
        embed_mesh(n)

    loaded("s4", "s6", "s5", "s7", "n1")
    for k in (4, 6, 5, 7):
        centre(k)

    g_copies["e", 1].wait_recv()
    g_copies["twin_e"].start()
    g_copies["w", 1].wait_recv()
    g_copies["twin_w"].start()
    pl.when(y != 1)(g_copies["e", 0].wait_recv)
    pl.when(y != 2)(g_copies["w", 0].wait_recv)
    for name in ("twin", "twin_e", "twin_w"):
        g_copies[name].wait_recv()

    @pl.when(has_far)
    def _():
        g_copies["far_e"].wait_recv()
        g_copies["far_w"].wait_recv()

    @pl.loop(0, 6 // GGROUP)
    def _(n):
        update(n * GGROUP, GGROUP, g2m_src, g2m_dst, 4, g_pre, g_pick, g_scat, gt, acc_h)

    def m_at(r, c, b):
        return mt.at[(r * 3 + c) * 3 + b]

    m_on, m_off = 2 * (1 - par), 2 * par
    m_copies = {}
    for b in range(3):
        m_copies["e", b] = remote(("me", b), m_at(1, 1, b), m_at(1, 0, b), east)
        m_copies["w", b] = remote(("mw", b), m_at(1, 1, b), m_at(1, 2, b), west)
        m_copies["far", b] = remote(("mfar", b), m_at(1, 1, b), m_at(m_on, 1, b), far)
        m_copies["twin", b] = remote(("mtwin", b), m_at(1, 1, b), m_at(m_off, 1, b), twin)
        m_copies["far_e", b] = remote(("mfe", b), m_at(m_off, 1, b), m_at(m_off, 0, b), east)
        m_copies["far_w", b] = remote(("mfw", b), m_at(m_off, 1, b), m_at(m_off, 2, b), west)
        m_copies["twin_e", b] = remote(("mte", b), m_at(1, 0, b), m_at(m_off, 0, b), twin)
        m_copies["twin_w", b] = remote(("mtw", b), m_at(1, 2, b), m_at(m_off, 2, b), twin)

    m_diag_e = [remote(("mfe", b), m_at(1, 1, b), m_at(m_on, 0, b), diag_e, ("md", b)) for b in range(3)]
    m_side_w = [remote(("mfe", b), m_at(1, 0, b), m_at(m_on, 0, b), far, ("ms", b)) for b in range(3)]
    m_side_e = [remote(("mfw", b), m_at(1, 2, b), m_at(m_on, 2, b), far, ("ms", b)) for b in range(3)]
    m_diag_w = [remote(("mfw", b), m_at(1, 1, b), m_at(m_on, 2, b), diag_w, ("md", b)) for b in range(3)]

    half = pl.ds(pl.multiple_of(par * 256, 256), 256)
    unit = mt.at[NEAR + chip, pl.ds(pl.multiple_of(lon * 16, 16), 16), half]
    c_unit = [remote(("cu", t), unit, unit, mate) for t, mate in enumerate(plane_mates)]
    z = chip // 2

    def plane(t):
        return mt.at[pl.ds(NEAR + 2 * lax.rem(z + t, 4), 2), :, half]

    c_z = [remote(("cz", t), plane(0), plane(0), mate) for t, mate in enumerate(z_mates)]
    c_twin = [remote(("cc", t), plane(t), plane(t), twin) for t in range(4)]

    def coarse_out():
        m_copies["twin", 0].wait_recv()
        mine = mt[12, 0:16].astype(F32)[0:COARSE]
        other = mt[(m_on * 3 + 1) * 3, 0:16].astype(F32)[0:COARSE]
        top = jnp.where(par == 0, mine, other)
        low = jnp.where(par == 0, other, mine)
        both = jnp.concatenate([top, low], axis=0)
        unit[...] = jnp.where(par == 0, both[:, 0:256], both[:, 256:512]).astype(BF)
        for copy in c_unit:
            copy.start()

    def patch_out(b):
        pl.when(has_far)(m_copies["far", b].start)
        pl.when(is_y[3])(m_diag_e[b].start)
        pl.when(is_y[0])(m_diag_w[b].start)
        m_copies["e", b].start()
        m_copies["w", b].start()

    g2m_round = (acc_g[...] + acc_h[...] * gain(4)).astype(BF)
    node_w = nf_v[0, 512:1024]
    for b in range(3):
        rows = slice(b * BLK, (b + 1) * BLK)
        u = npre[rows] + mm(g2m_round[rows], node_w)
        step = unit_rows(mm(silu(u), sec_v[6])) * gain(6)
        one = (start_v[rows].astype(F32) + step).astype(BF)
        one_v[rows] = one
        mt[12 + b] = mm(one, ef_v[1, 512:1024]).astype(BF)

        m_copies["twin", b].start()
        if b == 1:
            coarse_out()
            patch_out(0)
        if b >= 1:
            patch_out(b)

    one = one_v[...]
    dproj[...] = mm(one, ef_v[1, 1024:1536]).astype(BF).reshape(3, BLK, 512)
    npre[...] = mm(one, nf_v[1, 0:512])

    def corners(b):
        pl.when(has_far)(m_copies["far", b].wait_recv)
        pl.when(inner)(m_copies["far_e", b].start)
        pl.when(inner)(m_copies["far_w", b].start)
        pl.when(y == 1)(m_copies["e", b].wait_recv)
        pl.when(is_y[1])(m_side_w[b].start)
        pl.when(y == 2)(m_copies["w", b].wait_recv)
        pl.when(is_y[2])(m_side_e[b].start)

    groups = 24 // GROUP

    pl.loop(EARLY, EARLY + 2)(embed_mesh)
    for copy in c_unit:
        copy.wait_recv()
    for t in (0, 2, 1):
        c_z[t].start()
    c_twin[0].start()
    pl.when(inner)(functools.partial(corners, 0))
    pl.loop(EARLY + 2, EARLY + 3)(embed_mesh)
    pl.when(inner)(functools.partial(corners, 1))
    pl.loop(EARLY + 3, groups)(embed_mesh)
    pl.when(inner)(functools.partial(corners, 2))
    for b in range(3):
        @pl.when(jnp.logical_not(inner))
        def _(b=b):
            corners(b)

        if b:
            m_copies["twin", b].wait_recv()
        pl.when(y != 1)(m_copies["e", b].wait_recv)
        m_copies["twin_e", b].start()
        pl.when(y != 2)(m_copies["w", b].wait_recv)
        m_copies["twin_w", b].start()
    for t in (0, 2, 1):
        c_z[t].wait_recv()
        c_twin[3 - t].start()
    for b in range(3):
        m_copies["twin_e", b].wait_recv()
        m_copies["twin_w", b].wait_recv()
        pl.when(has_far)(m_copies["far_e", b].wait_recv)
        pl.when(has_far)(m_copies["far_w", b].wait_recv)
    for copy in c_twin:
        copy.wait_recv()

    @pl.loop(0, 24 // UGROUP)
    def _(n):
        update(n * UGROUP, UGROUP, mesh_src, mesh_dst, 5, m_pre, m_pick, m_scat, mt, acc_m)

    mesh_round = (acc_e[...] + acc_m[...] * gain(5)).astype(BF)
    u = npre[...] + mm(mesh_round, nf_v[1, 512:1024])
    step = unit_rows(mm(silu(u), sec_v[7])) * gain(7)
    out[0, 0] = (one_v[...].astype(F32) + step).astype(BF)

    pl.when(outer)(g_diag_e.wait_send)
    pl.when(inner)(g_side_e.wait_send)
    for b in range(3):
        pl.when(outer)(m_diag_e[b].wait_send)
        pl.when(inner)(m_side_e[b].wait_send)
    for name, copy in list(g_copies.items()) + list(m_copies.items()):
        kind = name if isinstance(name, str) else name[0]
        if kind == "far":
            pl.when(has_far)(copy.wait_send)
        elif kind.startswith("far"):
            pl.when(inner)(copy.wait_send)
        else:
            copy.wait_send()
    for copy in c_unit + c_z + c_twin:
        copy.wait_send()


def per_device(
    grid_feat,
    mesh_feat,
    g2m_feat,
    g2m_src,
    g2m_dst,
    g2m_rows,
    g2m_mask,
    g2m_live,
    mesh_efeat,
    mesh_src,
    mesh_dst,
    mesh_rows,
    mesh_mask,
    grid_in,
    mesh_in,
    edge_in,
    edge_first,
    node_first,
    second,
    norm_gains,
):
    hbm = pl.BlockSpec(memory_space=pl.ANY)
    vmem = pl.BlockSpec(memory_space=pltpu.VMEM)
    g2m_mask = jnp.swapaxes(g2m_mask, 1, 2)
    small = (
        mesh_feat,
        g2m_feat,
        g2m_rows,
        g2m_mask,
        mesh_efeat,
        mesh_rows,
        mesh_mask,
        mesh_in,
        edge_in,
        norm_gains,
    )
    scalars = (g2m_src, g2m_dst, g2m_live, mesh_src, mesh_dst)
    copies = 96
    return pl.pallas_call(
        kernel,
        out_shape=jax.ShapeDtypeStruct((1, 1, 384, 512), BF),
        in_specs=[hbm] * 20,
        out_specs=vmem,
        scratch_shapes=[pltpu.VMEM(x.shape, x.dtype) for x in small]
        + [pltpu.SMEM(x.shape, x.dtype) for x in scalars]
        + [
            pltpu.VMEM((2, 2, BLK, 474), BF),
            pltpu.VMEM((474, 512), BF),
            pltpu.VMEM((8, 512, 512), BF),
            pltpu.VMEM((2, 1536, 512), BF),
            pltpu.VMEM((2, 1024, 512), BF),
            pltpu.VMEM((16, BLK, 512), BF),
            pltpu.VMEM((NEAR + 8, BLK, 512), BF),
            pltpu.VMEM((384, 512), BF),
            pltpu.VMEM((384, 512), BF),
            pltpu.VMEM((3, BLK, 512), BF),
            pltpu.VMEM((384, 512), F32),
            pltpu.VMEM((6, BLK, 512), F32),
            pltpu.VMEM((6, BLK, 256), BF),
            pltpu.VMEM((6, 384, BLK), BF),
            pltpu.VMEM((24, BLK, 512), F32),
            pltpu.VMEM((24, BLK, 256), BF),
            pltpu.VMEM((24, 384, BLK), BF),
            pltpu.VMEM((384, 512), F32),
            pltpu.VMEM((384, 512), F32),
            pltpu.VMEM((384, 512), F32),
            pltpu.VMEM((384, 512), F32),
            pltpu.SemaphoreType.DMA((32,)),
            pltpu.SemaphoreType.DMA((copies,)),
            pltpu.SemaphoreType.DMA((copies,)),
        ],
        compiler_params=pltpu.CompilerParams(
            collective_id=0, has_side_effects=True, vmem_limit_bytes=56 * 1024 * 1024
        ),
        cost_estimate=pl.CostEstimate(flops=13 * 10**9, bytes_accessed=12 * 2**20, transcendentals=0),
    )(
        grid_feat,
        grid_in,
        second,
        edge_first,
        node_first,
        *small,
        *scalars,
    )


def solution(mesh):
    tile = lambda rank: P("lat", "lon", *([None] * (rank - 2)))
    in_specs = tuple(tile(r) for r in (4, 4, 5, 3, 3, 5, 4, 2, 5, 3, 3, 5, 4)) + (P(),) * 7
    return jax.shard_map(
        per_device, mesh=mesh, in_specs=in_specs, out_specs=tile(4), check_vma=False
    )
```

```python
import functools

import jax
import jax.numpy as jnp
from jax import lax
from jax.experimental import pallas as pl
from jax.experimental.pallas import tpu as pltpu
from jax.sharding import PartitionSpec as P

BF = jnp.bfloat16
F32 = jnp.float32
MESH = pl.DeviceIdType.MESH
BLK = 128
GROUP = 4
UGROUP = 12
GGROUP = 6
EARLY = 2
NEAR = 27
COARSE = 8


def mm(a, b):
    return jnp.dot(a, b, preferred_element_type=F32)


def silu(x):
    half = 0.5 * x
    return (half * jnp.tanh(half) + half).astype(BF)


def unit_rows(v):
    return v * lax.rsqrt(jnp.mean(v * v, axis=-1, keepdims=True) + 1e-05)


def kernel(
    grid_feat,
    grid_in,
    second,
    edge_first,
    node_first,
    mesh_feat_h,
    g2m_feat_h,
    g2m_rows_h,
    g2m_mask_h,
    mesh_efeat_h,
    mesh_rows_h,
    mesh_mask_h,
    mesh_in_h,
    edge_in_h,
    norm_gains_h,
    g2m_src_h,
    g2m_dst_h,
    g2m_live_h,
    mesh_src_h,
    mesh_dst_h,
    out,
    mesh_feat,
    g2m_feat,
    g2m_rows,
    g2m_mask,
    mesh_efeat,
    mesh_rows,
    mesh_mask,
    mesh_in,
    edge_in,
    norm_gains,
    g2m_src,
    g2m_dst,
    g2m_live,
    mesh_src,
    mesh_dst,
    feat_v,
    gin_v,
    sec_v,
    ef_v,
    nf_v,
    gt,
    mt,
    start_v,
    one_v,
    dproj,
    npre,
    g_pre,
    g_pick,
    g_scat,
    m_pre,
    m_pick,
    m_scat,
    acc_e,
    acc_m,
    acc_g,
    acc_h,
    load_sem,
    send_sem,
    recv_sem,
):
    lat, lon = lax.axis_index("lat"), lax.axis_index("lon")
    n_lat, n_lon = lax.axis_size("lat"), lax.axis_size("lon")
    par = lax.rem(lat, 2)
    chip = lat // 2
    east = (lat, lax.rem(lon + 1, n_lon))
    west = (lat, lax.rem(lon + n_lon - 1, n_lon))
    twin = (lat + 1 - 2 * par, lon)
    far_lat = lat + 2 * par - 1
    has_far = jnp.logical_and(far_lat >= 0, far_lat < n_lat)
    far = (far_lat, lon)
    y = lax.rem(lon, 4)
    diag_e, diag_w = (far_lat, east[1]), (far_lat, west[1])
    is_y = [jnp.logical_and(has_far, y == k) for k in range(4)]
    inner = jnp.logical_and(has_far, jnp.logical_or(y == 1, y == 2))
    outer = jnp.logical_and(has_far, jnp.logical_or(y == 0, y == 3))
    x_lat = lat + 2 - 4 * lax.rem(chip, 2)
    plane_mates = [(lat, lax.rem(lon + t, n_lon)) for t in range(1, n_lon)]
    plane_mates += [(x_lat, lax.rem(lon + t, n_lon)) for t in range(n_lon)]
    z_mates = [(lax.rem(lat + 4 * t, n_lat), lon) for t in range(1, n_lat // 4)]

    loads = {}

    def load(name, src, dst):
        copy = pltpu.make_async_copy(src, dst, load_sem.at[len(loads)])
        copy.start()
        loads[name] = copy

    def loaded(*names):
        for name in names:
            loads[name].wait()

    load("feat", grid_feat, feat_v)
    load("gin", grid_in, gin_v)
    load("s0", second.at[0], sec_v.at[0])
    load("gains", norm_gains_h, norm_gains)
    load("e0s", edge_first.at[0, pl.ds(512, 512)], ef_v.at[0, pl.ds(512, 512)])

    barrier = pltpu.get_barrier_semaphore()
    mates = plane_mates + [twin] + z_mates
    for mate in mates:
        pl.semaphore_signal(barrier, inc=1, device_id=mate, device_id_type=MESH)

    @pl.when(has_far)
    def _():
        pl.semaphore_signal(barrier, inc=1, device_id=far, device_id_type=MESH)

    for needed, diag in ((is_y[3], diag_e), (is_y[0], diag_w)):

        @pl.when(needed)
        def _(diag=diag):
            pl.semaphore_signal(barrier, inc=1, device_id=diag, device_id_type=MESH)

    load("e0d", edge_first.at[0, pl.ds(1024, 512)], ef_v.at[0, pl.ds(1024, 512)])
    load("e0e", edge_first.at[0, pl.ds(0, 512)], ef_v.at[0, pl.ds(0, 512)])
    load("mesh_feat", mesh_feat_h, mesh_feat)
    load("mesh_in", mesh_in_h, mesh_in)
    load("s1", second.at[1], sec_v.at[1])
    load("s2", second.at[2], sec_v.at[2])
    load("edge_in", edge_in_h, edge_in)
    for name, source, target in (
        ("g2m_feat", g2m_feat_h, g2m_feat),
        ("g2m_rows", g2m_rows_h, g2m_rows),
        ("g2m_mask", g2m_mask_h, g2m_mask),
        ("g2m_src", g2m_src_h, g2m_src),
        ("g2m_dst", g2m_dst_h, g2m_dst),
        ("g2m_live", g2m_live_h, g2m_live),
    ):
        load(name, source, target)
    load("n0", node_first.at[0], nf_v.at[0])
    for name, source, target in (
        ("mesh_efeat", mesh_efeat_h, mesh_efeat),
        ("mesh_rows", mesh_rows_h, mesh_rows),
        ("mesh_mask", mesh_mask_h, mesh_mask),
        ("mesh_src", mesh_src_h, mesh_src),
        ("mesh_dst", mesh_dst_h, mesh_dst),
    ):
        load(name, source, target)
    load("s3", second.at[3], sec_v.at[3])
    load("e1", edge_first.at[1], ef_v.at[1])
    load("s4", second.at[4], sec_v.at[4])
    load("s6", second.at[6], sec_v.at[6])
    load("s5", second.at[5], sec_v.at[5])
    load("n1", node_first.at[1], nf_v.at[1])
    load("s7", second.at[7], sec_v.at[7])

    peers = jnp.where(has_far, 1, 0) + jnp.where(outer, 1, 0)
    def gain(k):
        return norm_gains[...].astype(F32)[k : k + 1]

    def centre(k):
        w = sec_v[k].astype(F32)
        sec_v[k] = (w - jnp.mean(w, axis=-1, keepdims=True)).astype(BF)

    numbers = {}

    def remote(name, src, dst, device, sender=None):
        index = numbers.setdefault(name, len(numbers))
        leave = numbers.setdefault(sender or name, len(numbers))
        return pltpu.make_async_remote_copy(
            src_ref=src,
            dst_ref=dst,
            send_sem=send_sem.at[leave],
            recv_sem=recv_sem.at[index],
            device_id=device,
            device_id_type=MESH,
        )

    def g_at(r, c, n=1):
        return gt.at[pl.ds(r * 4 + c, n)]

    on_row, off_row = 3 * (1 - par), 3 * par
    g_rows = (1 + par, 2 - par)
    g_copies = {}
    for t in range(2):
        g_copies["e", t] = remote(("ge", t), g_at(g_rows[t], 2), g_at(g_rows[t], 0), east)
        g_copies["w", t] = remote(("gw", t), g_at(g_rows[t], 1), g_at(g_rows[t], 3), west)
    g_copies["far"] = remote("gfar", g_at(g_rows[0], 1, 2), g_at(on_row, 1, 2), far)
    g_copies["twin"] = remote("gtwin", g_at(g_rows[1], 1, 2), g_at(off_row, 1, 2), twin)
    g_copies["far_e"] = remote("gfe", g_at(off_row, 2), g_at(off_row, 0), east)
    g_copies["far_w"] = remote("gfw", g_at(off_row, 1), g_at(off_row, 3), west)
    g_diag_e = remote("gfe", g_at(g_rows[0], 2), g_at(on_row, 0), diag_e, "gdiag")
    g_side_w = remote("gfe", g_at(g_rows[0], 0), g_at(on_row, 0), far, "gside")
    g_side_e = remote("gfw", g_at(g_rows[0], 3), g_at(on_row, 3), far, "gside")
    g_diag_w = remote("gfw", g_at(g_rows[0], 1), g_at(on_row, 3), diag_w, "gdiag")
    g_copies["twin_e"] = remote("gte", g_at(g_rows[1], 0), g_at(off_row, 0), twin)
    g_copies["twin_w"] = remote("gtw", g_at(g_rows[1], 3), g_at(off_row, 3), twin)

    @pl.when(jnp.logical_not(has_far))
    def _():
        gt[pl.ds(off_row * 4, 4)] = jnp.zeros((4, BLK, 512), BF)
        mt[pl.ds(2 * par * 9, 9)] = jnp.zeros((9, BLK, 512), BF)

    loaded("feat", "gin", "s0", "gains")
    centre(0)
    w_in = gin_v[...]
    for t in range(2):
        x = feat_v[g_rows[t] - 1].reshape(2 * BLK, -1)
        v = mm(silu(mm(x, w_in)), sec_v[0])
        latent = (unit_rows(v) * gain(0)).astype(BF)
        if t == 0:
            loaded("e0s")
        proj = mm(latent, ef_v[0, 512:1024]).astype(BF)
        gt[pl.ds(g_rows[t] * 4 + 1, 2)] = proj.reshape(2, BLK, 512)
        if t == 0:
            pl.semaphore_wait(barrier, len(mates) + peers)

            @pl.when(has_far)
            def _():
                g_copies["far"].start()

            pl.when(is_y[3])(g_diag_e.start)
            pl.when(is_y[0])(g_diag_w.start)

        else:
            g_copies["twin"].start()
        g_copies["e", t].start()
        g_copies["w", t].start()

    loaded("s1", "mesh_feat", "mesh_in", "e0d", "e0e")
    centre(1)
    u = lax.dot_general(
        mesh_feat[0, 0], mesh_in[...], (((0,), (0,)), ((), ())), preferred_element_type=F32
    )
    start = (unit_rows(mm(silu(u), sec_v[1])) * gain(1)).astype(BF)
    start_v[...] = start
    dproj[...] = mm(start, ef_v[0, 1024:1536]).astype(BF).reshape(3, BLK, 512)
    loaded("n0")
    npre[...] = mm(start, nf_v[0, 0:512])

    def embed(base, count, feat, rows, mask, src, dst, live, layer, k, pre, pick, scat, acc, far_blocks):
        w_edge = edge_in[layer]
        hidden = []
        scatters = []
        spot = lax.broadcasted_iota(jnp.int32, (BLK, BLK), 0)
        place = lax.broadcasted_iota(jnp.int32, (3 * BLK, BLK), 0)
        for q in range(count):
            s = base + q
            u = lax.dot_general(
                feat[0, 0, s], w_edge, (((0,), (0,)), ((), ())), preferred_element_type=F32
            )
            hidden.append(silu(u))
            pair = rows[0, 0, s]
            hs, hd = pair[0:1], pair[1:2]
            if far_blocks:
                moved = ((hs >> 3) & 7) * 16 + (hs >> 6) * 8 + (hs & 7)
                is_coarse = jnp.where(src[0, 0, s] >= NEAR, 1, 0)
                hs = hs + is_coarse * (moved - hs)
            pick_s = jnp.where(spot == hs, 1.0, 0.0).T.astype(BF)
            pick_d = jnp.where(spot == hd, 1.0, 0.0).T.astype(BF)
            pick[s] = jnp.concatenate([pick_s, pick_d], axis=1)
            if live is None:
                keep = mask[0, 0, pl.ds(s, 1), :]
            else:
                keep = mask[0, s] * jnp.where(s < live, 1, 0)
            target = jnp.where(keep != 0, hd + BLK * dst[0, 0, s], -1)
            one = jnp.where(place == target, 1.0, 0.0).astype(BF)
            scat[s] = one
            scatters.append(one)
        e = (unit_rows(mm(jnp.concatenate(hidden, axis=0), sec_v[k])) * gain(k)).astype(BF)
        pre[pl.ds(base, count)] = mm(e, ef_v[layer, 0:512]).reshape(count, BLK, 512)
        acc[...] += mm(jnp.concatenate(scatters, axis=1), e)

    def update(base, count, src, dst, k, pre, pick, scat, table, acc):
        hidden = []
        for q in range(count):
            s = base + q
            blocks = jnp.concatenate([table[src[0, 0, s]], dproj[dst[0, 0, s]]], axis=0)
            hidden.append(silu(pre[s] + mm(pick[s], blocks)))
        message = unit_rows(mm(jnp.concatenate(hidden, axis=0), sec_v[k])).astype(BF)
        scatters = jnp.concatenate([scat[base + q] for q in range(count)], axis=1)
        acc[...] += mm(scatters, message)

    zeros = jnp.zeros(acc_e.shape, F32)
    acc_e[...] = zeros
    acc_m[...] = zeros
    acc_g[...] = zeros
    acc_h[...] = zeros
    loaded("s2", "edge_in", "g2m_feat", "g2m_rows", "g2m_mask", "g2m_src", "g2m_dst", "g2m_live")
    live = g2m_live[0, 0]
    centre(2)

    @pl.loop(0, 6 // GGROUP)
    def _(n):
        embed(
            n * GGROUP, GGROUP, g2m_feat, g2m_rows, g2m_mask, g2m_src, g2m_dst, live,
            0, 2, g_pre, g_pick, g_scat, acc_g, False,
        )

    pl.when(has_far)(g_copies["far"].wait_recv)
    pl.when(inner)(g_copies["far_e"].start)
    pl.when(inner)(g_copies["far_w"].start)
    pl.when(y == 1)(g_copies["e", 0].wait_recv)
    pl.when(is_y[1])(g_side_w.start)
    pl.when(y == 2)(g_copies["w", 0].wait_recv)
    pl.when(is_y[2])(g_side_e.start)

    loaded("s3", "e1", "mesh_efeat", "mesh_rows", "mesh_mask", "mesh_src", "mesh_dst")
    centre(3)

    def embed_mesh(n):
        embed(
            n * GROUP, GROUP, mesh_efeat, mesh_rows, mesh_mask, mesh_src, mesh_dst, None,
            1, 3, m_pre, m_pick, m_scat, acc_e, True,
        )

    @pl.loop(0, EARLY)
    def _(n):
        embed_mesh(n)

    loaded("s4", "s6", "s5", "s7", "n1")
    for k in (4, 6, 5, 7):
        centre(k)

    g_copies["e", 1].wait_recv()
    g_copies["twin_e"].start()
    g_copies["w", 1].wait_recv()
    g_copies["twin_w"].start()
    pl.when(y != 1)(g_copies["e", 0].wait_recv)
    pl.when(y != 2)(g_copies["w", 0].wait_recv)
    for name in ("twin", "twin_e", "twin_w"):
        g_copies[name].wait_recv()

    @pl.when(has_far)
    def _():
        g_copies["far_e"].wait_recv()
        g_copies["far_w"].wait_recv()

    @pl.loop(0, 6 // GGROUP)
    def _(n):
        update(n * GGROUP, GGROUP, g2m_src, g2m_dst, 4, g_pre, g_pick, g_scat, gt, acc_h)

    def m_at(r, c, b):
        return mt.at[(r * 3 + c) * 3 + b]

    m_on, m_off = 2 * (1 - par), 2 * par
    m_copies = {}
    for b in range(3):
        m_copies["e", b] = remote(("me", b), m_at(1, 1, b), m_at(1, 0, b), east)
        m_copies["w", b] = remote(("mw", b), m_at(1, 1, b), m_at(1, 2, b), west)
        m_copies["far", b] = remote(("mfar", b), m_at(1, 1, b), m_at(m_on, 1, b), far)
        m_copies["twin", b] = remote(("mtwin", b), m_at(1, 1, b), m_at(m_off, 1, b), twin)
        m_copies["far_e", b] = remote(("mfe", b), m_at(m_off, 1, b), m_at(m_off, 0, b), east)
        m_copies["far_w", b] = remote(("mfw", b), m_at(m_off, 1, b), m_at(m_off, 2, b), west)
        m_copies["twin_e", b] = remote(("mte", b), m_at(1, 0, b), m_at(m_off, 0, b), twin)
        m_copies["twin_w", b] = remote(("mtw", b), m_at(1, 2, b), m_at(m_off, 2, b), twin)

    m_diag_e = [remote(("mfe", b), m_at(1, 1, b), m_at(m_on, 0, b), diag_e, ("md", b)) for b in range(3)]
    m_side_w = [remote(("mfe", b), m_at(1, 0, b), m_at(m_on, 0, b), far, ("ms", b)) for b in range(3)]
    m_side_e = [remote(("mfw", b), m_at(1, 2, b), m_at(m_on, 2, b), far, ("ms", b)) for b in range(3)]
    m_diag_w = [remote(("mfw", b), m_at(1, 1, b), m_at(m_on, 2, b), diag_w, ("md", b)) for b in range(3)]

    half = pl.ds(pl.multiple_of(par * 256, 256), 256)
    unit = mt.at[NEAR + chip, pl.ds(pl.multiple_of(lon * 16, 16), 16), half]
    c_unit = [remote(("cu", t), unit, unit, mate) for t, mate in enumerate(plane_mates)]
    z = chip // 2

    def plane(t):
        return mt.at[pl.ds(NEAR + 2 * lax.rem(z + t, 4), 2), :, half]

    c_z = [remote(("cz", t), plane(0), plane(0), mate) for t, mate in enumerate(z_mates)]
    c_twin = [remote(("cc", t), plane(t), plane(t), twin) for t in range(4)]

    def coarse_out():
        m_copies["twin", 0].wait_recv()
        mine = mt[12, 0:16].astype(F32)[0:COARSE]
        other = mt[(m_on * 3 + 1) * 3, 0:16].astype(F32)[0:COARSE]
        top = jnp.where(par == 0, mine, other)
        low = jnp.where(par == 0, other, mine)
        both = jnp.concatenate([top, low], axis=0)
        unit[...] = jnp.where(par == 0, both[:, 0:256], both[:, 256:512]).astype(BF)
        for copy in c_unit:
            copy.start()

    def patch_out(b):
        pl.when(has_far)(m_copies["far", b].start)
        pl.when(is_y[3])(m_diag_e[b].start)
        pl.when(is_y[0])(m_diag_w[b].start)
        m_copies["e", b].start()
        m_copies["w", b].start()

    g2m_round = (acc_g[...] + acc_h[...] * gain(4)).astype(BF)
    node_w = nf_v[0, 512:1024]
    for b in range(3):
        rows = slice(b * BLK, (b + 1) * BLK)
        u = npre[rows] + mm(g2m_round[rows], node_w)
        step = unit_rows(mm(silu(u), sec_v[6])) * gain(6)
        one = (start_v[rows].astype(F32) + step).astype(BF)
        one_v[rows] = one
        mt[12 + b] = mm(one, ef_v[1, 512:1024]).astype(BF)

        m_copies["twin", b].start()
        if b == 1:
            coarse_out()
            patch_out(0)
        if b >= 1:
            patch_out(b)

    one = one_v[...]
    dproj[...] = mm(one, ef_v[1, 1024:1536]).astype(BF).reshape(3, BLK, 512)
    npre[...] = mm(one, nf_v[1, 0:512])

    def corners(b):
        pl.when(has_far)(m_copies["far", b].wait_recv)
        pl.when(inner)(m_copies["far_e", b].start)
        pl.when(inner)(m_copies["far_w", b].start)
        pl.when(y == 1)(m_copies["e", b].wait_recv)
        pl.when(is_y[1])(m_side_w[b].start)
        pl.when(y == 2)(m_copies["w", b].wait_recv)
        pl.when(is_y[2])(m_side_e[b].start)

    groups = 24 // GROUP

    pl.loop(EARLY, EARLY + 2)(embed_mesh)
    for copy in c_unit:
        copy.wait_recv()
    for t in (0, 2, 1):
        c_z[t].start()
    c_twin[0].start()
    pl.when(inner)(functools.partial(corners, 0))
    pl.loop(EARLY + 2, EARLY + 3)(embed_mesh)
    pl.when(inner)(functools.partial(corners, 1))
    pl.loop(EARLY + 3, groups)(embed_mesh)
    pl.when(inner)(functools.partial(corners, 2))
    for b in range(3):
        @pl.when(jnp.logical_not(inner))
        def _(b=b):
            corners(b)

        if b:
            m_copies["twin", b].wait_recv()
        pl.when(y != 1)(m_copies["e", b].wait_recv)
        m_copies["twin_e", b].start()
        pl.when(y != 2)(m_copies["w", b].wait_recv)
        m_copies["twin_w", b].start()
    for t in (0, 2, 1):
        c_z[t].wait_recv()
        c_twin[3 - t].start()
    for b in range(3):
        m_copies["twin_e", b].wait_recv()
        m_copies["twin_w", b].wait_recv()
        pl.when(has_far)(m_copies["far_e", b].wait_recv)
        pl.when(has_far)(m_copies["far_w", b].wait_recv)
    for copy in c_twin:
        copy.wait_recv()

    @pl.loop(0, 24 // UGROUP)
    def _(n):
        update(n * UGROUP, UGROUP, mesh_src, mesh_dst, 5, m_pre, m_pick, m_scat, mt, acc_m)

    mesh_round = (acc_e[...] + acc_m[...] * gain(5)).astype(BF)
    u = npre[...] + mm(mesh_round, nf_v[1, 512:1024])
    step = unit_rows(mm(silu(u), sec_v[7])) * gain(7)
    out[0, 0] = (one_v[...].astype(F32) + step).astype(BF)

    pl.when(outer)(g_diag_e.wait_send)
    pl.when(inner)(g_side_e.wait_send)
    for b in range(3):
        pl.when(outer)(m_diag_e[b].wait_send)
        pl.when(inner)(m_side_e[b].wait_send)
    for name, copy in list(g_copies.items()) + list(m_copies.items()):
        kind = name if isinstance(name, str) else name[0]
        if kind == "far":
            pl.when(has_far)(copy.wait_send)
        elif kind.startswith("far"):
            pl.when(inner)(copy.wait_send)
        else:
            copy.wait_send()
    for copy in c_unit + c_z + c_twin:
        copy.wait_send()


def per_device(
    grid_feat,
    mesh_feat,
    g2m_feat,
    g2m_src,
    g2m_dst,
    g2m_rows,
    g2m_mask,
    g2m_live,
    mesh_efeat,
    mesh_src,
    mesh_dst,
    mesh_rows,
    mesh_mask,
    grid_in,
    mesh_in,
    edge_in,
    edge_first,
    node_first,
    second,
    norm_gains,
):
    hbm = pl.BlockSpec(memory_space=pl.ANY)
    vmem = pl.BlockSpec(memory_space=pltpu.VMEM)
    g2m_mask = jnp.swapaxes(g2m_mask, 1, 2)
    small = (
        mesh_feat,
        g2m_feat,
        g2m_rows,
        g2m_mask,
        mesh_efeat,
        mesh_rows,
        mesh_mask,
        mesh_in,
        edge_in,
        norm_gains,
    )
    scalars = (g2m_src, g2m_dst, g2m_live, mesh_src, mesh_dst)
    copies = 96
    return pl.pallas_call(
        kernel,
        out_shape=jax.ShapeDtypeStruct((1, 1, 384, 512), BF),
        in_specs=[hbm] * 20,
        out_specs=vmem,
        scratch_shapes=[pltpu.VMEM(x.shape, x.dtype) for x in small]
        + [pltpu.SMEM(x.shape, x.dtype) for x in scalars]
        + [
            pltpu.VMEM((2, 2, BLK, 474), BF),
            pltpu.VMEM((474, 512), BF),
            pltpu.VMEM((8, 512, 512), BF),
            pltpu.VMEM((2, 1536, 512), BF),
            pltpu.VMEM((2, 1024, 512), BF),
            pltpu.VMEM((16, BLK, 512), BF),
            pltpu.VMEM((NEAR + 8, BLK, 512), BF),
            pltpu.VMEM((384, 512), BF),
            pltpu.VMEM((384, 512), BF),
            pltpu.VMEM((3, BLK, 512), BF),
            pltpu.VMEM((384, 512), F32),
            pltpu.VMEM((6, BLK, 512), F32),
            pltpu.VMEM((6, BLK, 256), BF),
            pltpu.VMEM((6, 384, BLK), BF),
            pltpu.VMEM((24, BLK, 512), F32),
            pltpu.VMEM((24, BLK, 256), BF),
            pltpu.VMEM((24, 384, BLK), BF),
            pltpu.VMEM((384, 512), F32),
            pltpu.VMEM((384, 512), F32),
            pltpu.VMEM((384, 512), F32),
            pltpu.VMEM((384, 512), F32),
            pltpu.SemaphoreType.DMA((32,)),
            pltpu.SemaphoreType.DMA((copies,)),
            pltpu.SemaphoreType.DMA((copies,)),
        ],
        compiler_params=pltpu.CompilerParams(
            collective_id=0, has_side_effects=True, vmem_limit_bytes=56 * 1024 * 1024
        ),
        cost_estimate=pl.CostEstimate(flops=13 * 10**9, bytes_accessed=12 * 2**20, transcendentals=0),
    )(
        grid_feat,
        grid_in,
        second,
        edge_first,
        node_first,
        *small,
        *scalars,
    )


def solution(mesh):
    tile = lambda rank: P("lat", "lon", *([None] * (rank - 2)))
    in_specs = tuple(tile(r) for r in (4, 4, 5, 3, 3, 5, 4, 2, 5, 3, 3, 5, 4)) + (P(),) * 7
    return jax.shard_map(
        per_device, mesh=mesh, in_specs=in_specs, out_specs=tile(4), check_vma=False
    )
```
